512 devices in a mesh: row: 16 (over x, z_hi, core), col: 32 (over y, z_lo).
Axes of the slice: x: 4, y: 8, z: 8 (z_hi: 2, z_lo: 4; z = z_hi * 4 + z_lo), core: 2. Of those that a mesh axis runs over, the one named last changes fastest.
Arguments:
- features: bfloat16 [65536, 128], P(('row', 'col')), may hold values from -6 to 6
- cotangent: bfloat16 [65536, 128], P(('row', 'col')), may hold values from -6 to 6
- self_weight: bfloat16 [128, 128], replicated, may hold values from -0.5 to 0.5
- neighbour_weight: bfloat16 [128, 128], replicated, may hold values from -0.5 to 0.5
- shift_bias: float32 [128], replicated, may hold values from -3 to 3
- tile_rows: int32 [16, 32, 128], P('row', 'col'), may hold values from 0 to 31, as said below
- tile_cols: int32 [16, 32, 128], P('row', 'col'), may hold values from 0 to 15
- edge_targets: int32 [16, 32, 128, 128], P('row', 'col'), may hold values from -1 to 127, as said below
- edge_sources: int32 [16, 32, 128, 128], P('row', 'col'), may hold values from -1 to 127
Outputs:
- activations: bfloat16 [65536, 128], P(('row', 'col'))
- feature_grad: bfloat16 [65536, 128], P(('row', 'col'))
- self_grad: float32 [128, 128], replicated
- neighbour_grad: float32 [128, 128], replicated
- bias_grad: float32 [128], replicated
The draws below stay inside these ranges and needn't reach their ends.
Inputs may be any that keep to these rules, and one draw needn't show every extreme that they name: `tile_rows`: each device has 128 block slots; the live ones come first, at least one per device, and on some device all 128 are live. Live counts differ strongly from device to device. A live slot holds 1 to 128 edges in its first positions, the rest -1; some slot holds exactly 128; an empty slot is all -1. edge_sources is -1 exactly where edge_targets is.
All inputs are finite; a program needn't handle non-finite values.
Results may differ from the reference program's by a relative error of at most 0.0075.
Values may be sent and summed in bfloat16 or wider, within the bound.
A program may use at most 64 MiB of HBM per device.

```python
import jax
import jax.numpy as jnp
from jax import lax

F = 128
TILE = 128
NODES_DEV = 128
EDGES = 128
SLOTS = 128
NODES = 65536
N_ROW = 16
N_COL = 32


def edge_counts(key):
    devices_all = N_ROW * N_COL
    first, second, third = jax.random.split(key, 3)
    lowest = max(SLOTS // 4, 1)
    live = jax.random.randint(first, (devices_all,), lowest, SLOTS + 1)
    chosen = jax.random.randint(second, (), 0, devices_all)
    live = jnp.where(jnp.arange(devices_all) == chosen, SLOTS, live)
    sizes = jax.random.randint(third, (devices_all, SLOTS), 1, EDGES + 1)
    sizes = sizes.at[chosen, 0].set(EDGES)
    slot_pos = jnp.arange(SLOTS)
    counts = jnp.where(slot_pos[None, :] < live[:, None], sizes, 0)
    return counts.reshape(N_ROW, N_COL, SLOTS)


def draw_edge_targets(key, part):
    counts = edge_counts(key)
    key = jax.random.fold_in(key, 11)
    local = jax.random.randint(key, (N_ROW, N_COL, SLOTS, EDGES), 0, TILE)
    position = jnp.arange(EDGES)
    return jnp.where(position < counts[..., None], local, -1).astype(jnp.int32)


def draw_edge_sources(key, part):
    counts = edge_counts(key)
    key = jax.random.fold_in(key, 12)
    local = jax.random.randint(key, (N_ROW, N_COL, SLOTS, EDGES), 0, TILE)
    position = jnp.arange(EDGES)
    return jnp.where(position < counts[..., None], local, -1).astype(jnp.int32)


def draw_tile_rows(key, part):
    key = jax.random.fold_in(key, 13)
    return jax.random.randint(key, (N_ROW, N_COL, SLOTS), 0, N_COL * NODES_DEV // TILE).astype(jnp.int32)


def draw_tile_cols(key, part):
    key = jax.random.fold_in(key, 17)
    return jax.random.randint(key, (N_ROW, N_COL, SLOTS), 0, N_ROW * NODES_DEV // TILE).astype(jnp.int32)


def steps_of(own_key, dims, shards, low, top_value):
    loudness = 1.0
    for dim, shards_of in shards:
        heights = jax.random.uniform(jax.random.fold_in(jax.random.fold_in(own_key, 6), dim), (shards_of,), jnp.float32, low / len(shards), top_value / len(shards))
        loudness = loudness * jnp.repeat(jnp.exp(heights), dims[dim] // shards_of).reshape((-1,) + (1,) * (len(dims) - 1 - dim))
    return loudness


def gaussian(own_key, dims, deviation, bound, pieces=(), held_as=jnp.bfloat16):
    drawn = deviation * jax.random.normal(own_key, dims, jnp.float32)
    if pieces:
        drawn = drawn * steps_of(own_key, dims, pieces, -0.22, 0.18)
    return jnp.clip(drawn, -bound, bound).astype(held_as)


def setup_inputs(seed: int = 0) -> dict:
    key_of = jax.random.split(jax.random.key(seed), 10)
    return {
        "features": gaussian(key_of[0], (NODES, F), 1.0, 6.0, ((0, 512),)),
        "cotangent": gaussian(key_of[1], (NODES, F), 1.0, 6.0, ((0, 512),)),
        "self_weight": gaussian(key_of[2], (F, F), F ** -0.5, 0.5),
        "neighbour_weight": gaussian(key_of[3], (F, F), F ** -0.5, 0.5),
        "shift_bias": gaussian(key_of[4], (F,), 0.5, 3.0, (), jnp.float32),
        "tile_rows": draw_tile_rows(jax.random.fold_in(key_of[9], 71), 0),
        "tile_cols": draw_tile_cols(jax.random.fold_in(key_of[9], 71), 0),
        "edge_targets": draw_edge_targets(jax.random.fold_in(key_of[9], 71), 0),
        "edge_sources": draw_edge_sources(jax.random.fold_in(key_of[9], 71), 0),
    }


def reference(features, cotangent, self_weight, neighbour_weight, shift_bias, tile_rows, tile_cols, edge_targets, edge_sources):
    shape_all = edge_targets.shape
    row_pos = lax.broadcasted_iota(jnp.int32, shape_all, 0)
    col_pos = lax.broadcasted_iota(jnp.int32, shape_all, 1)
    usable = (edge_targets >= 0).astype(jnp.float32)
    dest_index = row_pos * (N_COL * NODES_DEV) + tile_rows[..., None] * TILE + jnp.maximum(edge_targets, 0)
    within = tile_cols[..., None] * TILE + jnp.maximum(edge_sources, 0)
    source_index = ((within // NODES_DEV) * N_COL + col_pos) * NODES_DEV + within % NODES_DEV
    dest_flat = dest_index.reshape(N_ROW * N_COL, -1).astype(jnp.int32)
    source_flat = source_index.reshape(N_ROW * N_COL, -1).astype(jnp.int32)
    weight_flat = usable.reshape(N_ROW * N_COL, -1)
    degree = jnp.zeros((NODES,), jnp.float32).at[dest_flat.reshape(-1)].add(weight_flat.reshape(-1))

    def forward_step(total, item):
        dest, source, weight = item
        return total.at[dest].add(features[source].astype(jnp.float32) * weight[:, None]), None

    summed, _ = lax.scan(forward_step, jnp.zeros((NODES, F), jnp.float32), (dest_flat, source_flat, weight_flat))
    divisor = (degree + 1.0)[:, None]
    aggregate = (summed / divisor).astype(jnp.bfloat16)
    preact = jnp.dot(features, self_weight, preferred_element_type=jnp.float32)
    preact = preact + jnp.dot(aggregate, neighbour_weight, preferred_element_type=jnp.float32) + shift_bias
    sigma = jax.nn.sigmoid(preact)
    activations = (preact * sigma).astype(jnp.bfloat16)
    grad_pre = (cotangent.astype(jnp.float32) * sigma * (1.0 + preact * (1.0 - sigma))).astype(jnp.bfloat16)
    scaling = NODES ** -0.5
    self_grad = jnp.dot(features.T, grad_pre, preferred_element_type=jnp.float32) * scaling
    neighbour_grad = jnp.dot(aggregate.T, grad_pre, preferred_element_type=jnp.float32) * scaling
    bias_grad = jnp.sum(grad_pre.astype(jnp.float32), axis=0) * scaling
    scaled_grad = (jnp.dot(grad_pre, neighbour_weight.T, preferred_element_type=jnp.float32) / divisor).astype(jnp.bfloat16)

    def backward_step(total, item):
        dest, source, weight = item
        return total.at[source].add(scaled_grad[dest].astype(jnp.float32) * weight[:, None]), None

    back_sum, _ = lax.scan(backward_step, jnp.zeros((NODES, F), jnp.float32), (dest_flat, source_flat, weight_flat))
    feature_grad = (jnp.dot(grad_pre, self_weight.T, preferred_element_type=jnp.float32) + back_sum).astype(jnp.bfloat16)
    return (activations, feature_grad, self_grad, neighbour_grad, bias_grad)
```

```python
import functools

import jax
import jax.numpy as jnp
from jax import lax
from jax.experimental import pallas as pl
from jax.experimental.pallas import tpu as pltpu
from jax.sharding import PartitionSpec as P

TILE = 128
HALF = TILE // 2
CORES = 2
UNROLL = 8
MESH = pl.DeviceIdType.MESH
F32 = jnp.float32
BF16 = jnp.bfloat16
LANES = (((1,), (1,)), ((), ()))
ROWS = (((0,), (0,)), ((), ()))


def far_first(n):
    return sorted(range(1, n), key=lambda d: -min(d, n - d))


def layer_kernel(
    sizes,
    feat,
    cot,
    ws,
    wn,
    bias,
    trow,
    tcol,
    et,
    es,
    act_o,
    fg_o,
    sg_o,
    ng_o,
    bg_o,
    fwd_adj,
    bwd_adj,
    runs,
    slot_counts,
    meta_v,
    meta_s,
    xb,
    pa,
    pb,
    ra,
    rb,
    sa,
    sb,
    ra2,
    rb2,
    deg,
    deg_r,
    deg2,
    deg2_r,
    ga,
    gb,
    bp,
    br,
    bs,
    br2,
    wl,
    wc,
    w1,
    wx,
    w2,
    wy,
    w3,
    wz,
    wo,
    send_sems,
    recv_sems,
    meta_sem,
):
    n_q, n_y, n_z, slots, scaling = sizes
    r = lax.axis_index("row")
    c = lax.axis_index("col")
    q, k = r // CORES, r % CORES
    y, z = c // n_z, c % n_z
    n_src = n_q * CORES
    n_dst = n_y * n_z
    wrows = TILE // n_q

    def at_y(d):
        return (r, lax.rem(y + d, n_y) * n_z + z)

    def at_z(d):
        return (r, y * n_z + lax.rem(z + d, n_z))

    def at_q(d):
        return (lax.rem(q + d, n_q) * CORES + k, c)

    sibling = (q * CORES + 1 - k, c)

    used = [0]
    started = []

    def send(src, dst, device):
        i = used[0]
        used[0] += 1
        copy = pltpu.make_async_remote_copy(
            src_ref=src,
            dst_ref=dst,
            send_sem=send_sems.at[i],
            recv_sem=recv_sems.at[i],
            device_id=device,
            device_id_type=MESH,
        )
        copy.start()
        started.append(copy)
        return copy

    def arrive(copies):
        for copy in copies:
            copy.wait_recv()

    y_far, z_far, q_far = far_first(n_y), far_first(n_z), far_first(n_q)

    barrier = pltpu.get_barrier_semaphore()
    partners = [at_y(d) for d in y_far] + [at_z(d) for d in z_far]
    partners += [at_q(d) for d in q_far] + [sibling]
    for partner in partners:
        pl.semaphore_signal(barrier, inc=1, device_id=partner, device_id_type=MESH)

    sub = lax.broadcasted_iota(jnp.int32, (TILE, TILE), 0)
    lane = lax.broadcasted_iota(jnp.int32, (TILE, TILE), 1)
    rows_l = jnp.broadcast_to(trow[...], (TILE, TILE))
    cols_l = jnp.broadcast_to(tcol[...], (TILE, TILE))
    rows_s, cols_s = rows_l.T, cols_l.T

    def order(ids_l, ids_s, other_s):
        before = (ids_l < ids_s) | ((ids_l == ids_s) & (lane < sub))
        rank = jnp.sum(before.astype(jnp.int32), axis=1, keepdims=True)
        same = jnp.sum(((ids_l == ids_s) & (lane < sub)).astype(jnp.int32), axis=1, keepdims=True)
        packed = sub + other_s * 128 + jnp.minimum(same, 1) * 4096
        ordered = jnp.sum(jnp.where(rank == lane, packed, 0), axis=0, keepdims=True)
        upto = jnp.sum((ids_s <= lane).astype(jnp.int32), axis=0, keepdims=True)
        below = jnp.sum((ids_s < lane).astype(jnp.int32), axis=0, keepdims=True)
        ends = jnp.maximum(upto - 1, 0) + jnp.where(upto > below, 256, 0)
        return ordered, ends

    by_row, row_ends = order(rows_l, rows_s, cols_s)
    by_col, col_ends = order(cols_l, cols_s, rows_s)
    zero_row = jnp.zeros_like(by_row)
    meta_v[...] = jnp.concatenate([by_row, row_ends, by_col, col_ends] + [zero_row] * 4, axis=0)
    meta_copy = pltpu.make_async_copy(meta_v, meta_s, meta_sem)
    meta_copy.start()

    def build(g, _):
        base = pl.multiple_of(g * UNROLL, UNROLL)
        targets = et[pl.ds(base, UNROLL), :]
        sources = es[pl.ds(base, UNROLL), :]
        counts = []
        for u in range(UNROLL):
            hot_t = jnp.where(sub == targets[u : u + 1, :], 1.0, 0.0).astype(BF16)
            hot_s = jnp.where(sub == sources[u : u + 1, :], 1.0, 0.0).astype(BF16)
            fwd = lax.dot_general(hot_t, hot_s, LANES, preferred_element_type=F32)
            bwd = lax.dot_general(hot_s, hot_t, LANES, preferred_element_type=F32)
            fwd_adj[base + u] = fwd.astype(BF16)
            bwd_adj[base + u] = bwd.astype(BF16)
            counts.append(jnp.sum(bwd, axis=0, keepdims=True))
        slot_counts[pl.ds(base, UNROLL), :] = jnp.concatenate(counts, axis=0)
        return 0

    lax.fori_loop(0, slots // UNROLL, build, 0)

    xb[k * n_q + q] = feat[...]
    pl.semaphore_wait(barrier, len(partners))

    mine = xb.at[k * n_q + q]
    x_copies = [send(mine, mine, at_q(d)) for d in q_far]

    tile_sub = lax.broadcasted_iota(jnp.int32, (n_y * 8, TILE), 0)
    wanted = (tile_sub // 8) * n_z + tile_sub % 8
    hits = (jnp.broadcast_to(trow[...], (n_y * 8, TILE)) == wanted) & (tile_sub % 8 < n_z)
    partial = jnp.dot(
        jnp.where(hits, 1.0, 0.0).astype(BF16),
        slot_counts[...].astype(BF16),
        preferred_element_type=F32,
    )
    deg[...] = partial.reshape(n_y, 8, TILE)
    deg_copies = [send(deg.at[lax.rem(y + d, n_y)], deg_r.at[d], at_y(d)) for d in y_far]
    self_term = jnp.dot(feat[...], ws[...], preferred_element_type=F32)

    meta_copy.wait()
    arrive(x_copies)
    half_block = xb.at[pl.ds(k * n_q, n_q)]
    x_core = send(half_block, half_block, sibling)
    arrive(deg_copies)
    summed = deg[y]
    for d in range(1, n_y):
        summed = summed + deg_r[d]
    deg2[...] = summed
    deg2_copies = [send(deg2, deg2_r.at[d], at_z(d)) for d in z_far]
    arrive([x_core])

    def forward(g, acc):
        for u in range(UNROLL):
            s = g * UNROLL + u
            word = meta_s[0, s]
            slot, col = word & 127, (word >> 7) & 31
            source = xb[(col & 1) * n_q + (col >> 1)]
            product = jnp.dot(fwd_adj[slot], source, preferred_element_type=F32)
            acc = jnp.where(word >= 4096, acc, 0.0) + product
            runs[s] = acc.astype(BF16)
        return acc

    lax.fori_loop(0, slots // UNROLL, forward, jnp.zeros((TILE, TILE), F32))

    def place_rows(i, _):
        word = meta_s[1, i]
        run = runs[word & 127]
        run = jnp.where(word >= 256, run, jnp.zeros_like(run))
        pa[i] = run[:HALF]
        pb[(i % n_z) * n_y + i // n_z] = run[HALF:]
        return 0

    lax.fori_loop(0, n_dst, place_rows, 0)

    a_copies = [
        send(pa.at[pl.ds(lax.rem(y + d, n_y) * n_z, n_z)], ra.at[d], at_y(d)) for d in y_far
    ]
    b_copies = [
        send(pb.at[pl.ds(lax.rem(z + d, n_z) * n_y, n_y)], rb.at[d], at_z(d)) for d in z_far
    ]

    arrive(deg2_copies)
    degree = deg2[...]
    for d in range(1, n_z):
        degree = degree + deg2_r[d]
    sub8 = lax.broadcasted_iota(jnp.int32, (8, TILE), 0)
    degree = jnp.sum(jnp.where(sub8 == z, degree, 0.0), axis=0, keepdims=True)
    inverse = 1.0 / (jnp.broadcast_to(degree, (TILE, TILE)).T + 1.0)

    arrive(a_copies)
    total = pa[pl.ds(y * n_z, n_z)].astype(F32)
    for d in range(1, n_y):
        total = total + ra[d].astype(F32)
    sa[...] = total.astype(BF16)
    a2_copies = [send(sa.at[lax.rem(z + d, n_z)], ra2.at[d], at_z(d)) for d in z_far]
    arrive(b_copies)
    total = pb[pl.ds(z * n_y, n_y)].astype(F32)
    for d in range(1, n_z):
        total = total + rb[d].astype(F32)
    sb[...] = total.astype(BF16)
    b2_copies = [send(sb.at[lax.rem(y + d, n_y)], rb2.at[d], at_y(d)) for d in y_far]
    arrive(a2_copies)
    upper = sa[z].astype(F32)
    for d in range(1, n_z):
        upper = upper + ra2[d].astype(F32)
    arrive(b2_copies)
    lower = sb[y].astype(F32)
    for d in range(1, n_y):
        lower = lower + rb2[d].astype(F32)
    neighbour_sum = jnp.concatenate([upper, lower], axis=0)

    aggregate = (neighbour_sum * inverse).astype(BF16)
    preact = self_term + jnp.dot(aggregate, wn[...], preferred_element_type=F32) + bias[...]
    sigma = jax.nn.sigmoid(preact)
    grad_pre = (cot[...].astype(F32) * sigma * (1.0 + preact * (1.0 - sigma))).astype(BF16)
    scaled = lax.dot_general(grad_pre, wn[...], LANES, preferred_element_type=F32) * inverse
    scaled = scaled.astype(BF16)

    ga[y * n_z + z] = scaled[:HALF]
    gb[z * n_y + y] = scaled[HALF:]
    own_a, own_b = ga.at[y * n_z + z], gb.at[z * n_y + y]
    b_copies = [send(own_b, own_b, at_y(d)) for d in y_far]
    a_copies = [send(own_a, own_a, at_z(d)) for d in z_far]

    act_o[...] = (preact * sigma).astype(BF16)
    self_local = lax.dot_general(feat[...], grad_pre, ROWS, preferred_element_type=F32)
    neighbour_local = lax.dot_general(aggregate, grad_pre, ROWS, preferred_element_type=F32)
    bias_local = jnp.sum(grad_pre.astype(F32).reshape(TILE // 8, 8, TILE), axis=0)
    wl[0, :TILE] = self_local
    wl[1, :TILE] = neighbour_local
    wl[0, TILE:] = bias_local
    wl[1, TILE:] = bias_local
    own_term = lax.dot_general(grad_pre, ws[...], LANES, preferred_element_type=F32)
    w_core = send(wl.at[1 - k], wc, sibling)

    arrive(a_copies)
    group_a = ga.at[pl.ds(y * n_z, n_z)]
    a_copies = [send(group_a, group_a, at_y(d)) for d in y_far]
    arrive(b_copies)
    group_b = gb.at[pl.ds(z * n_y, n_y)]
    b_copies = [send(group_b, group_b, at_z(d)) for d in z_far]

    arrive([w_core])
    both = wl[k] + wc[...]
    for j in range(n_q):
        w1[j] = jnp.concatenate([both[j * wrows : (j + 1) * wrows], both[TILE:]], axis=0)
    wx_copies = [send(w1.at[lax.rem(q + d, n_q)], wx.at[d], at_q(d)) for d in q_far]
    arrive(wx_copies)
    summed = w1[q]
    for d in range(1, n_q):
        summed = summed + wx[d]
    w2[...] = summed
    wy_copies = [send(w2, wy.at[d], at_y(d)) for d in y_far]

    arrive(a_copies)
    arrive(b_copies)

    def backward(g, acc):
        for u in range(UNROLL):
            s = g * UNROLL + u
            word = meta_s[2, s]
            slot, row = word & 127, (word >> 7) & 31
            target = jnp.concatenate([ga[row], gb[(row % n_z) * n_y + row // n_z]], axis=0)
            product = jnp.dot(bwd_adj[slot], target, preferred_element_type=F32)
            acc = jnp.where(word >= 4096, acc, 0.0) + product
            runs[s] = acc.astype(BF16)
        return acc

    lax.fori_loop(0, slots // UNROLL, backward, jnp.zeros((TILE, TILE), F32))

    def place_cols(j, _):
        word = meta_s[3, j]
        run = runs[word & 127]
        run = jnp.where(word >= 256, run, jnp.zeros_like(run))
        bp[(j % CORES) * n_q + j // CORES] = run
        return 0

    lax.fori_loop(0, n_src, place_cols, 0)

    b_core = send(bp.at[pl.ds((1 - k) * n_q, n_q)], br, sibling)
    arrive(wy_copies)
    summed = w2[...]
    for d in range(1, n_y):
        summed = summed + wy[d]
    w3[...] = summed
    wz_copies = [send(w3, wz.at[d], at_z(d)) for d in z_far]
    arrive([b_core])
    bs[...] = (bp[pl.ds(k * n_q, n_q)].astype(F32) + br[...].astype(F32)).astype(BF16)
    back_copies = [send(bs.at[lax.rem(q + d, n_q)], br2.at[d], at_q(d)) for d in q_far]

    arrive(wz_copies)
    summed = w3[...]
    for d in range(1, n_z):
        summed = summed + wz[d]
    summed = summed * scaling
    bg_o[...] = jnp.sum(summed[wrows:], axis=0, keepdims=True)
    wo[k * n_q + q] = summed[:wrows]
    own_w = wo.at[k * n_q + q]
    wo_copies = [send(own_w, own_w, at_q(d)) for d in q_far]

    arrive(back_copies)
    feature_grad = own_term + bs[q].astype(F32)
    for d in range(1, n_q):
        feature_grad = feature_grad + br2[d].astype(F32)
    fg_o[...] = feature_grad.astype(BF16)

    arrive(wo_copies)
    own_half = wo.at[pl.ds(k * n_q, n_q)]
    arrive([send(own_half, own_half, sibling)])
    sg_o[...] = wo[pl.ds(0, n_q)].reshape(TILE, TILE)
    ng_o[...] = wo[pl.ds(n_q, n_q)].reshape(TILE, TILE)
    for copy in started:
        copy.wait_send()


def on_device(
    n_row,
    n_col,
    features,
    cotangent,
    self_weight,
    neighbour_weight,
    shift_bias,
    tile_rows,
    tile_cols,
    edge_targets,
    edge_sources,
):
    slots = edge_targets.shape[2]
    n_z = 4 if n_col >= 16 else 2
    n_y, n_q = n_col // n_z, n_row // CORES
    scaling = float((TILE * n_row * n_col) ** (-0.5))
    sizes = (n_q, n_y, n_z, slots, scaling)
    wrows = TILE // n_q
    n_dst, n_src = n_col, n_row
    copies = 7 * (n_y - 1) + 6 * (n_z - 1) + 4 * (n_q - 1) + 4
    scratch = [
        pltpu.VMEM((slots, TILE, TILE), BF16),
        pltpu.VMEM((slots, TILE, TILE), BF16),
        pltpu.VMEM((slots, TILE, TILE), BF16),
        pltpu.VMEM((slots, TILE), F32),
        pltpu.VMEM((8, TILE), jnp.int32),
        pltpu.SMEM((8, TILE), jnp.int32),
        pltpu.VMEM((n_src, TILE, TILE), BF16),
        pltpu.VMEM((n_dst, HALF, TILE), BF16),
        pltpu.VMEM((n_dst, HALF, TILE), BF16),
        pltpu.VMEM((n_y, n_z, HALF, TILE), BF16),
        pltpu.VMEM((n_z, n_y, HALF, TILE), BF16),
        pltpu.VMEM((n_z, HALF, TILE), BF16),
        pltpu.VMEM((n_y, HALF, TILE), BF16),
        pltpu.VMEM((n_z, HALF, TILE), BF16),
        pltpu.VMEM((n_y, HALF, TILE), BF16),
        pltpu.VMEM((n_y, 8, TILE), F32),
        pltpu.VMEM((n_y, 8, TILE), F32),
        pltpu.VMEM((8, TILE), F32),
        pltpu.VMEM((n_z, 8, TILE), F32),
        pltpu.VMEM((n_dst, HALF, TILE), BF16),
        pltpu.VMEM((n_dst, HALF, TILE), BF16),
        pltpu.VMEM((n_src, TILE, TILE), BF16),
        pltpu.VMEM((n_q, TILE, TILE), BF16),
        pltpu.VMEM((n_q, TILE, TILE), BF16),
        pltpu.VMEM((n_q, TILE, TILE), BF16),
        pltpu.VMEM((CORES, TILE + 8, TILE), F32),
        pltpu.VMEM((TILE + 8, TILE), F32),
        pltpu.VMEM((n_q, wrows + 8, TILE), F32),
        pltpu.VMEM((n_q, wrows + 8, TILE), F32),
        pltpu.VMEM((wrows + 8, TILE), F32),
        pltpu.VMEM((n_y, wrows + 8, TILE), F32),
        pltpu.VMEM((wrows + 8, TILE), F32),
        pltpu.VMEM((n_z, wrows + 8, TILE), F32),
        pltpu.VMEM((CORES * n_q, wrows, TILE), F32),
        pltpu.SemaphoreType.DMA((copies,)),
        pltpu.SemaphoreType.DMA((copies,)),
        pltpu.SemaphoreType.DMA,
    ]
    whole = pl.BlockSpec(memory_space=pltpu.VMEM)
    act, fg, sg, ng, bg = pl.pallas_call(
        functools.partial(layer_kernel, sizes),
        out_shape=(
            jax.ShapeDtypeStruct((TILE, TILE), BF16),
            jax.ShapeDtypeStruct((TILE, TILE), BF16),
            jax.ShapeDtypeStruct((TILE, TILE), F32),
            jax.ShapeDtypeStruct((TILE, TILE), F32),
            jax.ShapeDtypeStruct((1, TILE), F32),
        ),
        in_specs=[whole] * 9,
        out_specs=(whole,) * 5,
        scratch_shapes=scratch,
        compiler_params=pltpu.CompilerParams(
            collective_id=0, has_side_effects=True, vmem_limit_bytes=44 * 2**20
        ),
        name="sage_layer",
    )(
        features,
        cotangent,
        self_weight,
        neighbour_weight,
        shift_bias.reshape(1, TILE),
        tile_rows.reshape(1, slots),
        tile_cols.reshape(1, slots),
        edge_targets.reshape(slots, -1),
        edge_sources.reshape(slots, -1),
    )
    return act, fg, sg, ng, bg.reshape(TILE)


def solution(mesh):
    in_specs = (
        P(("row", "col"), None),
        P(("row", "col"), None),
        P(),
        P(),
        P(),
        P("row", "col", None),
        P("row", "col", None),
        P("row", "col", None, None),
        P("row", "col", None, None),
    )
    out_specs = (P(("row", "col"), None), P(("row", "col"), None), P(), P(), P())
    body = functools.partial(on_device, mesh.shape["row"], mesh.shape["col"])
    return jax.shard_map(
        body, mesh=mesh, in_specs=in_specs, out_specs=out_specs, check_vma=False
    )
```

```python
import functools

import jax
import jax.numpy as jnp
from jax import lax
from jax.experimental import pallas as pl
from jax.experimental.pallas import tpu as pltpu
from jax.sharding import PartitionSpec as P

TILE = 128
HALF = TILE // 2
CORES = 2
UNROLL = 8
MESH = pl.DeviceIdType.MESH
F32 = jnp.float32
BF16 = jnp.bfloat16
LANES = (((1,), (1,)), ((), ()))
ROWS = (((0,), (0,)), ((), ()))


def far_first(n):
    return sorted(range(1, n), key=lambda d: -min(d, n - d))


def layer_kernel(
    sizes,
    feat_h,
    cot_h,
    ws_h,
    wn_h,
    bias_h,
    trow_h,
    tcol_h,
    et_h,
    es_h,
    act_o,
    fg_o,
    sg_o,
    ng_o,
    bg_o,
    feat,
    cot,
    ws,
    wn,
    bias,
    trow,
    tcol,
    et,
    es,
    act_v,
    fg_v,
    bg_v,
    fwd_adj,
    bwd_adj,
    runs,
    slot_counts,
    meta_v,
    meta_s,
    xb,
    pa,
    pb,
    ra,
    rb,
    sa,
    sb,
    ra2,
    rb2,
    deg,
    deg_r,
    deg2,
    deg2_r,
    ga,
    gb,
    bp,
    br,
    bs,
    br2,
    wl,
    wc,
    w1,
    wx,
    w2,
    wy,
    w3,
    wz,
    wo,
    send_sems,
    recv_sems,
    meta_sem,
    in_sems,
    out_sems,
):
    n_q, n_y, n_z, slots, scaling = sizes
    r = lax.axis_index("row")
    c = lax.axis_index("col")
    q, k = r // CORES, r % CORES
    y, z = c // n_z, c % n_z
    n_src = n_q * CORES
    n_dst = n_y * n_z
    wrows = TILE // n_q

    def at_y(d):
        return (r, lax.rem(y + d, n_y) * n_z + z)

    def at_z(d):
        return (r, y * n_z + lax.rem(z + d, n_z))

    def at_q(d):
        return (lax.rem(q + d, n_q) * CORES + k, c)

    sibling = (q * CORES + 1 - k, c)

    used = [0]
    started = []

    def send(src, dst, device):
        i = used[0]
        used[0] += 1
        copy = pltpu.make_async_remote_copy(
            src_ref=src,
            dst_ref=dst,
            send_sem=send_sems.at[i],
            recv_sem=recv_sems.at[i],
            device_id=device,
            device_id_type=MESH,
        )
        copy.start()
        started.append(copy)
        return copy

    def arrive(copies):
        for copy in copies:
            copy.wait_recv()

    y_far, z_far, q_far = far_first(n_y), far_first(n_z), far_first(n_q)

    local_in = []
    for i, (far, near) in enumerate(
        zip(
            (trow_h, tcol_h, feat_h, et_h, es_h, ws_h, wn_h, bias_h, cot_h),
            (trow, tcol, feat, et, es, ws, wn, bias, cot),
        )
    ):
        local_in.append(pltpu.make_async_copy(far, near, in_sems.at[i]))
        local_in[-1].start()

    local_out = []

    def put(src, dst):
        copy = pltpu.make_async_copy(src, dst, out_sems.at[len(local_out)])
        copy.start()
        local_out.append(copy)

    barrier = pltpu.get_barrier_semaphore()
    partners = [at_y(d) for d in y_far] + [at_z(d) for d in z_far]
    partners += [at_q(d) for d in q_far] + [sibling]
    for partner in partners:
        pl.semaphore_signal(barrier, inc=1, device_id=partner, device_id_type=MESH)

    for copy in local_in[:2]:
        copy.wait()

    sub = lax.broadcasted_iota(jnp.int32, (TILE, TILE), 0)
    lane = lax.broadcasted_iota(jnp.int32, (TILE, TILE), 1)
    rows_l = jnp.broadcast_to(trow[...], (TILE, TILE))
    cols_l = jnp.broadcast_to(tcol[...], (TILE, TILE))
    rows_s, cols_s = rows_l.T, cols_l.T

    def order(ids_l, ids_s, other_s):
        before = (ids_l < ids_s) | ((ids_l == ids_s) & (lane < sub))
        rank = jnp.sum(before.astype(jnp.int32), axis=1, keepdims=True)
        same = jnp.sum(((ids_l == ids_s) & (lane < sub)).astype(jnp.int32), axis=1, keepdims=True)
        packed = sub + other_s * 128 + jnp.minimum(same, 1) * 4096
        ordered = jnp.sum(jnp.where(rank == lane, packed, 0), axis=0, keepdims=True)
        upto = jnp.sum((ids_s <= lane).astype(jnp.int32), axis=0, keepdims=True)
        below = jnp.sum((ids_s < lane).astype(jnp.int32), axis=0, keepdims=True)
        ends = jnp.maximum(upto - 1, 0) + jnp.where(upto > below, 256, 0)
        return ordered, ends

    by_row, row_ends = order(rows_l, rows_s, cols_s)
    by_col, col_ends = order(cols_l, cols_s, rows_s)
    zero_row = jnp.zeros_like(by_row)
    meta_v[...] = jnp.concatenate([by_row, row_ends, by_col, col_ends] + [zero_row] * 4, axis=0)
    meta_copy = pltpu.make_async_copy(meta_v, meta_s, meta_sem)
    meta_copy.start()

    local_in[2].wait()
    xb[k * n_q + q] = feat[...]
    pl.semaphore_wait(barrier, len(partners))

    mine = xb.at[k * n_q + q]
    x_copies = {d: send(mine, mine, at_q(d)) for d in q_far}
    x_core = [send(mine, mine, sibling)]
    for copy in local_in[3:]:
        copy.wait()

    def build(g, _):
        base = pl.multiple_of(g * UNROLL, UNROLL)
        targets = et[pl.ds(base, UNROLL), :]
        sources = es[pl.ds(base, UNROLL), :]
        counts = []
        for u in range(UNROLL):
            hot_t = jnp.where(sub == targets[u : u + 1, :], 1.0, 0.0).astype(BF16)
            hot_s = jnp.where(sub == sources[u : u + 1, :], 1.0, 0.0).astype(BF16)
            fwd = lax.dot_general(hot_t, hot_s, LANES, preferred_element_type=F32)
            bwd = lax.dot_general(hot_s, hot_t, LANES, preferred_element_type=F32)
            fwd_adj[base + u] = fwd.astype(BF16)
            bwd_adj[base + u] = bwd.astype(BF16)
            counts.append(jnp.sum(bwd, axis=0, keepdims=True))
        slot_counts[pl.ds(base, UNROLL), :] = jnp.concatenate(counts, axis=0)
        return 0

    lax.fori_loop(0, slots // UNROLL, build, 0)

    tile_sub = lax.broadcasted_iota(jnp.int32, (n_y * 8, TILE), 0)
    wanted = (tile_sub // 8) * n_z + tile_sub % 8
    hits = (jnp.broadcast_to(trow[...], (n_y * 8, TILE)) == wanted) & (tile_sub % 8 < n_z)
    partial = jnp.dot(
        jnp.where(hits, 1.0, 0.0).astype(BF16),
        slot_counts[...].astype(BF16),
        preferred_element_type=F32,
    )
    deg[...] = partial.reshape(n_y, 8, TILE)
    deg_copies = [send(deg.at[lax.rem(y + d, n_y)], deg_r.at[d], at_y(d)) for d in y_far]
    self_term = jnp.dot(feat[...], ws[...], preferred_element_type=F32)

    meta_copy.wait()
    for d in reversed(q_far):
        arrive([x_copies[d]])
        block = xb.at[k * n_q + lax.rem(q + n_q - d, n_q)]
        x_core.append(send(block, block, sibling))
    arrive(x_core)

    def forward(g, acc):
        for u in range(UNROLL):
            s = g * UNROLL + u
            word = meta_s[0, s]
            slot, col = word & 127, (word >> 7) & 31
            source = xb[(col & 1) * n_q + (col >> 1)]
            product = jnp.dot(fwd_adj[slot], source, preferred_element_type=F32)
            acc = jnp.where(word >= 4096, acc, 0.0) + product
            runs[s] = acc.astype(BF16)
        return acc

    lax.fori_loop(0, slots // UNROLL, forward, jnp.zeros((TILE, TILE), F32))

    def place_rows(i, _):
        word = meta_s[1, i]
        run = runs[word & 127]
        run = jnp.where(word >= 256, run, jnp.zeros_like(run))
        pa[i] = run[:HALF]
        pb[(i % n_z) * n_y + i // n_z] = run[HALF:]
        return 0

    lax.fori_loop(0, n_dst, place_rows, 0)

    a_copies = [
        send(pa.at[pl.ds(lax.rem(y + d, n_y) * n_z, n_z)], ra.at[d], at_y(d)) for d in y_far
    ]
    b_copies = [
        send(pb.at[pl.ds(lax.rem(z + d, n_z) * n_y, n_y)], rb.at[d], at_z(d)) for d in z_far
    ]

    arrive(deg_copies)
    summed = deg[y]
    for d in range(1, n_y):
        summed = summed + deg_r[d]
    deg2[...] = summed
    deg2_copies = [send(deg2, deg2_r.at[d], at_z(d)) for d in z_far]

    arrive(a_copies)
    total = pa[pl.ds(y * n_z, n_z)].astype(F32)
    for d in range(1, n_y):
        total = total + ra[d].astype(F32)
    sa[...] = total.astype(BF16)
    a2_copies = [send(sa.at[lax.rem(z + d, n_z)], ra2.at[d], at_z(d)) for d in z_far]

    arrive(deg2_copies)
    degree = deg2[...]
    for d in range(1, n_z):
        degree = degree + deg2_r[d]
    sub8 = lax.broadcasted_iota(jnp.int32, (8, TILE), 0)
    degree = jnp.sum(jnp.where(sub8 == z, degree, 0.0), axis=0, keepdims=True)
    inverse = 1.0 / (jnp.broadcast_to(degree, (TILE, TILE)).T + 1.0)

    arrive(b_copies)
    total = pb[pl.ds(z * n_y, n_y)].astype(F32)
    for d in range(1, n_z):
        total = total + rb[d].astype(F32)
    sb[...] = total.astype(BF16)
    b2_copies = [send(sb.at[lax.rem(y + d, n_y)], rb2.at[d], at_y(d)) for d in y_far]
    arrive(a2_copies)
    upper = sa[z].astype(F32)
    for d in range(1, n_z):
        upper = upper + ra2[d].astype(F32)
    arrive(b2_copies)
    lower = sb[y].astype(F32)
    for d in range(1, n_y):
        lower = lower + rb2[d].astype(F32)
    neighbour_sum = jnp.concatenate([upper, lower], axis=0)

    aggregate = (neighbour_sum * inverse).astype(BF16)
    preact = self_term + jnp.dot(aggregate, wn[...], preferred_element_type=F32) + bias[...]
    sigma = jax.nn.sigmoid(preact)
    grad_pre = (cot[...].astype(F32) * sigma * (1.0 + preact * (1.0 - sigma))).astype(BF16)
    scaled = lax.dot_general(grad_pre, wn[...], LANES, preferred_element_type=F32) * inverse
    scaled = scaled.astype(BF16)

    ga[y * n_z + z] = scaled[:HALF]
    gb[z * n_y + y] = scaled[HALF:]
    own_a, own_b = ga.at[y * n_z + z], gb.at[z * n_y + y]
    b_copies = [send(own_b, own_b, at_y(d)) for d in y_far]
    a_copies = [send(own_a, own_a, at_z(d)) for d in z_far]

    act_v[...] = (preact * sigma).astype(BF16)
    put(act_v, act_o)
    self_local = lax.dot_general(feat[...], grad_pre, ROWS, preferred_element_type=F32)
    neighbour_local = lax.dot_general(aggregate, grad_pre, ROWS, preferred_element_type=F32)
    bias_local = jnp.sum(grad_pre.astype(F32).reshape(TILE // 8, 8, TILE), axis=0)
    wl[0, :TILE] = self_local
    wl[1, :TILE] = neighbour_local
    wl[0, TILE:] = bias_local
    wl[1, TILE:] = bias_local
    own_term = lax.dot_general(grad_pre, ws[...], LANES, preferred_element_type=F32)
    w_core = send(wl.at[1 - k], wc, sibling)

    arrive([w_core])
    both = wl[k] + wc[...]
    for j in range(n_q):
        w1[j] = jnp.concatenate([both[j * wrows : (j + 1) * wrows], both[TILE:]], axis=0)
    wx_copies = [send(w1.at[lax.rem(q + d, n_q)], wx.at[d], at_q(d)) for d in q_far]

    arrive(a_copies)
    group_a = ga.at[pl.ds(y * n_z, n_z)]
    a_copies = [send(group_a, group_a, at_y(d)) for d in y_far]
    arrive(b_copies)
    group_b = gb.at[pl.ds(z * n_y, n_y)]
    b_copies = [send(group_b, group_b, at_z(d)) for d in z_far]

    arrive(wx_copies)
    summed = w1[q]
    for d in range(1, n_q):
        summed = summed + wx[d]
    w2[...] = summed
    wy_copies = [send(w2, wy.at[d], at_y(d)) for d in y_far]

    arrive(a_copies)
    arrive(b_copies)

    def backward(g, acc):
        for u in range(UNROLL):
            s = g * UNROLL + u
            word = meta_s[2, s]
            slot, row = word & 127, (word >> 7) & 31
            target = jnp.concatenate([ga[row], gb[(row % n_z) * n_y + row // n_z]], axis=0)
            product = jnp.dot(bwd_adj[slot], target, preferred_element_type=F32)
            acc = jnp.where(word >= 4096, acc, 0.0) + product
            runs[s] = acc.astype(BF16)
        return acc

    lax.fori_loop(0, slots // UNROLL, backward, jnp.zeros((TILE, TILE), F32))

    def place_cols(j, _):
        word = meta_s[3, j]
        run = runs[word & 127]
        run = jnp.where(word >= 256, run, jnp.zeros_like(run))
        bp[(j % CORES) * n_q + j // CORES] = run
        return 0

    lax.fori_loop(0, n_src, place_cols, 0)

    b_core = {}
    for d in q_far + [0]:
        i = lax.rem(q + d, n_q)
        b_core[d] = send(bp.at[(1 - k) * n_q + i], br.at[i], sibling)
    arrive(wy_copies)
    summed = w2[...]
    for d in range(1, n_y):
        summed = summed + wy[d]
    w3[...] = summed
    wz_copies = [send(w3, wz.at[d], at_z(d)) for d in z_far]
    back_copies = []
    for d in q_far:
        i = lax.rem(q + d, n_q)
        arrive([b_core[d]])
        bs[i] = (bp[k * n_q + i].astype(F32) + br[i].astype(F32)).astype(BF16)
        back_copies.append(send(bs.at[i], br2.at[d], at_q(d)))
    arrive([b_core[0]])
    feature_grad = own_term + (bp[k * n_q + q].astype(F32) + br[q].astype(F32))

    arrive(wz_copies)
    summed = w3[...]
    for d in range(1, n_z):
        summed = summed + wz[d]
    summed = summed * scaling
    wo[k * n_q + q] = summed[:wrows]
    own_w = wo.at[k * n_q + q]
    wo_copies = [send(own_w, own_w, at_q(d)) for d in q_far]
    bg_v[...] = jnp.sum(summed[wrows:], axis=0, keepdims=True)
    put(bg_v, bg_o)

    arrive(back_copies)
    for d in range(1, n_q):
        feature_grad = feature_grad + br2[d].astype(F32)
    fg_v[...] = feature_grad.astype(BF16)
    put(fg_v, fg_o)

    arrive(wo_copies)
    own_half = wo.at[pl.ds(k * n_q, n_q)]
    last = send(own_half, own_half, sibling)
    arrive([last])
    put(wo.at[pl.ds(0, n_q)], sg_o)
    put(wo.at[pl.ds(n_q, n_q)], ng_o)
    for copy in local_out:
        copy.wait()
    for copy in started:
        copy.wait_send()


def hand_over(*refs):
    sources, results, sems = refs[:5], refs[5:10], refs[10]
    copies = [
        pltpu.make_async_copy(source, result, sems.at[i])
        for i, (source, result) in enumerate(zip(sources, results))
    ]
    for copy in copies:
        copy.start()
    for copy in copies:
        copy.wait()


def on_device(
    n_row,
    n_col,
    features,
    cotangent,
    self_weight,
    neighbour_weight,
    shift_bias,
    tile_rows,
    tile_cols,
    edge_targets,
    edge_sources,
):
    slots = edge_targets.shape[2]
    n_z = 4 if n_col >= 16 else 2
    n_y, n_q = n_col // n_z, n_row // CORES
    scaling = float((TILE * n_row * n_col) ** (-0.5))
    sizes = (n_q, n_y, n_z, slots, scaling)
    wrows = TILE // n_q
    n_dst, n_src = n_col, n_row
    copies = 6 * (n_y - 1) + 6 * (n_z - 1) + 4 * (n_q - 1) + 2 * n_q + 2
    scratch = [
        pltpu.VMEM((TILE, TILE), BF16),
        pltpu.VMEM((TILE, TILE), BF16),
        pltpu.VMEM((TILE, TILE), BF16),
        pltpu.VMEM((TILE, TILE), BF16),
        pltpu.VMEM((1, TILE), F32),
        pltpu.VMEM((1, slots), jnp.int32),
        pltpu.VMEM((1, slots), jnp.int32),
        pltpu.VMEM((slots, TILE), jnp.int32),
        pltpu.VMEM((slots, TILE), jnp.int32),
        pltpu.VMEM((TILE, TILE), BF16),
        pltpu.VMEM((TILE, TILE), BF16),
        pltpu.VMEM((1, TILE), F32),
        pltpu.VMEM((slots, TILE, TILE), BF16),
        pltpu.VMEM((slots, TILE, TILE), BF16),
        pltpu.VMEM((slots, TILE, TILE), BF16),
        pltpu.VMEM((slots, TILE), F32),
        pltpu.VMEM((8, TILE), jnp.int32),
        pltpu.SMEM((8, TILE), jnp.int32),
        pltpu.VMEM((n_src, TILE, TILE), BF16),
        pltpu.VMEM((n_dst, HALF, TILE), BF16),
        pltpu.VMEM((n_dst, HALF, TILE), BF16),
        pltpu.VMEM((n_y, n_z, HALF, TILE), BF16),
        pltpu.VMEM((n_z, n_y, HALF, TILE), BF16),
        pltpu.VMEM((n_z, HALF, TILE), BF16),
        pltpu.VMEM((n_y, HALF, TILE), BF16),
        pltpu.VMEM((n_z, HALF, TILE), BF16),
        pltpu.VMEM((n_y, HALF, TILE), BF16),
        pltpu.VMEM((n_y, 8, TILE), F32),
        pltpu.VMEM((n_y, 8, TILE), F32),
        pltpu.VMEM((8, TILE), F32),
        pltpu.VMEM((n_z, 8, TILE), F32),
        pltpu.VMEM((n_dst, HALF, TILE), BF16),
        pltpu.VMEM((n_dst, HALF, TILE), BF16),
        pltpu.VMEM((n_src, TILE, TILE), BF16),
        pltpu.VMEM((n_q, TILE, TILE), BF16),
        pltpu.VMEM((n_q, TILE, TILE), BF16),
        pltpu.VMEM((n_q, TILE, TILE), BF16),
        pltpu.VMEM((CORES, TILE + 8, TILE), F32),
        pltpu.VMEM((TILE + 8, TILE), F32),
        pltpu.VMEM((n_q, wrows + 8, TILE), F32),
        pltpu.VMEM((n_q, wrows + 8, TILE), F32),
        pltpu.VMEM((wrows + 8, TILE), F32),
        pltpu.VMEM((n_y, wrows + 8, TILE), F32),
        pltpu.VMEM((wrows + 8, TILE), F32),
        pltpu.VMEM((n_z, wrows + 8, TILE), F32),
        pltpu.VMEM((CORES * n_q, wrows, TILE), F32),
        pltpu.SemaphoreType.DMA((copies,)),
        pltpu.SemaphoreType.DMA((copies,)),
        pltpu.SemaphoreType.DMA,
        pltpu.SemaphoreType.DMA((9,)),
        pltpu.SemaphoreType.DMA((5,)),
    ]
    whole = pl.BlockSpec(memory_space=pl.ANY)
    out_shape = (
        jax.ShapeDtypeStruct((TILE, TILE), BF16),
        jax.ShapeDtypeStruct((TILE, TILE), BF16),
        jax.ShapeDtypeStruct((n_q, wrows, TILE), F32),
        jax.ShapeDtypeStruct((n_q, wrows, TILE), F32),
        jax.ShapeDtypeStruct((1, TILE), F32),
    )
    results = pl.pallas_call(
        functools.partial(layer_kernel, sizes),
        out_shape=out_shape,
        in_specs=[pl.BlockSpec(memory_space=pltpu.HBM)] * 9,
        out_specs=(whole,) * 5,
        scratch_shapes=scratch,
        compiler_params=pltpu.CompilerParams(
            collective_id=0, has_side_effects=True, vmem_limit_bytes=60 * 2**20
        ),
        name="sage_layer",
    )(
        features,
        cotangent,
        self_weight,
        neighbour_weight,
        shift_bias.reshape(1, TILE),
        tile_rows.reshape(1, slots),
        tile_cols.reshape(1, slots),
        edge_targets.reshape(slots, -1),
        edge_sources.reshape(slots, -1),
    )
    act, fg, sg, ng, bg = pl.pallas_call(
        hand_over,
        out_shape=out_shape,
        in_specs=[pl.BlockSpec(memory_space=pltpu.VMEM)] * 5,
        out_specs=(pl.BlockSpec(memory_space=pltpu.HBM),) * 5,
        scratch_shapes=[pltpu.SemaphoreType.DMA((5,))],
        name="hand_over",
    )(*results)
    return act, fg, sg.reshape(TILE, TILE), ng.reshape(TILE, TILE), bg.reshape(TILE)


def solution(mesh):
    in_specs = (
        P(("row", "col"), None),
        P(("row", "col"), None),
        P(),
        P(),
        P(),
        P("row", "col", None),
        P("row", "col", None),
        P("row", "col", None, None),
        P("row", "col", None, None),
    )
    out_specs = (P(("row", "col"), None), P(("row", "col"), None), P(), P(), P())
    body = functools.partial(on_device, mesh.shape["row"], mesh.shape["col"])
    return jax.shard_map(
        body, mesh=mesh, in_specs=in_specs, out_specs=out_specs, check_vma=False
    )
```

```python
import functools

import jax
import jax.numpy as jnp
from jax import lax
from jax.experimental import pallas as pl
from jax.experimental.pallas import tpu as pltpu
from jax.sharding import PartitionSpec as P

TILE = 128
HALF = TILE // 2
CORES = 2
UNROLL = 16
MESH = pl.DeviceIdType.MESH
F32 = jnp.float32
BF16 = jnp.bfloat16
LANES = (((1,), (1,)), ((), ()))
ROWS = (((0,), (0,)), ((), ()))


def far_first(n):
    return sorted(range(1, n), key=lambda d: -min(d, n - d))


def layer_kernel(
    sizes,
    feat_h,
    cot_h,
    ws_h,
    wn_h,
    bias_h,
    trow_h,
    tcol_h,
    et_h,
    es_h,
    act_o,
    fg_o,
    sg_o,
    ng_o,
    bg_o,
    feat,
    cot,
    ws,
    wn,
    bias,
    trow,
    tcol,
    et,
    es,
    act_v,
    fg_v,
    bg_v,
    fwd_adj,
    bwd_adj,
    runs,
    slot_counts,
    meta_v,
    meta_s,
    xb,
    pa,
    pb,
    ra,
    rb,
    sa,
    sb,
    ra2,
    rb2,
    deg,
    deg_r,
    deg2,
    deg2_r,
    ga,
    gb,
    bp,
    br,
    bs,
    br2,
    wl,
    wc,
    w1,
    wx,
    w2,
    wy,
    w3,
    wz,
    wo,
    send_sems,
    recv_sems,
    meta_sem,
    in_sems,
    out_sems,
):
    n_q, n_y, n_z, slots, scaling = sizes
    r = lax.axis_index("row")
    c = lax.axis_index("col")
    q, k = r // CORES, r % CORES
    y, z = c // n_z, c % n_z
    n_src = n_q * CORES
    n_dst = n_y * n_z
    wrows = TILE // n_q

    def at_y(d):
        return (r, lax.rem(y + d, n_y) * n_z + z)

    def at_z(d):
        return (r, y * n_z + lax.rem(z + d, n_z))

    def at_q(d):
        return (lax.rem(q + d, n_q) * CORES + k, c)

    sibling = (q * CORES + 1 - k, c)

    used = [0]
    started = []

    def send(src, dst, device):
        i = used[0]
        used[0] += 1
        copy = pltpu.make_async_remote_copy(
            src_ref=src,
            dst_ref=dst,
            send_sem=send_sems.at[i],
            recv_sem=recv_sems.at[i],
            device_id=device,
            device_id_type=MESH,
        )
        copy.start()
        started.append(copy)
        return copy

    def arrive(copies):
        for copy in copies:
            copy.wait_recv()

    y_far, z_far, q_far = far_first(n_y), far_first(n_z), far_first(n_q)

    barrier = pltpu.get_barrier_semaphore()
    partners = [at_q(d) for d in q_far] + [at_y(d) for d in y_far]
    partners += [at_z(d) for d in z_far] + [sibling]
    for partner in partners:
        pl.semaphore_signal(barrier, inc=1, device_id=partner, device_id_type=MESH)

    local_in = []
    for i, (far, near) in enumerate(
        zip(
            (feat_h, trow_h, tcol_h, et_h, es_h, feat_h, ws_h, wn_h, bias_h, cot_h),
            (xb.at[k * n_q + q], trow, tcol, et, es, feat, ws, wn, bias, cot),
        )
    ):
        local_in.append(pltpu.make_async_copy(far, near, in_sems.at[i]))
        local_in[-1].start()

    local_out = []

    def put(src, dst):
        copy = pltpu.make_async_copy(src, dst, out_sems.at[len(local_out)])
        copy.start()
        local_out.append(copy)

    pl.semaphore_wait(barrier, len(partners))

    mine = xb.at[k * n_q + q]
    x_copies = {d: send(feat_h, mine, at_q(d)) for d in q_far}
    x_core = [send(feat_h, mine, sibling)]
    for copy in local_in:
        copy.wait()

    sub = lax.broadcasted_iota(jnp.int32, (TILE, TILE), 0)
    lane = lax.broadcasted_iota(jnp.int32, (TILE, TILE), 1)
    rows_l = jnp.broadcast_to(trow[...], (TILE, TILE))
    cols_l = jnp.broadcast_to(tcol[...], (TILE, TILE))
    rows_s, cols_s = rows_l.T, cols_l.T

    def order(ids_l, ids_s, other_s):
        before = (ids_l < ids_s) | ((ids_l == ids_s) & (lane < sub))
        rank = jnp.sum(before.astype(jnp.int32), axis=1, keepdims=True)
        same = jnp.sum(((ids_l == ids_s) & (lane < sub)).astype(jnp.int32), axis=1, keepdims=True)
        packed = sub + other_s * 128 + jnp.minimum(same, 1) * 4096
        ordered = jnp.sum(jnp.where(rank == lane, packed, 0), axis=0, keepdims=True)
        upto = jnp.sum((ids_s <= lane).astype(jnp.int32), axis=0, keepdims=True)
        below = jnp.sum((ids_s < lane).astype(jnp.int32), axis=0, keepdims=True)
        ends = jnp.maximum(upto - 1, 0) + jnp.where(upto > below, 256, 0)
        return ordered, ends

    by_row, row_ends = order(rows_l, rows_s, cols_s)
    by_col, col_ends = order(cols_l, cols_s, rows_s)
    zero_row = jnp.zeros_like(by_row)
    meta_v[...] = jnp.concatenate([by_row, row_ends, by_col, col_ends] + [zero_row] * 4, axis=0)
    meta_copy = pltpu.make_async_copy(meta_v, meta_s, meta_sem)
    meta_copy.start()


    def build(g, _):
        base = pl.multiple_of(g * UNROLL, UNROLL)
        targets = et[pl.ds(base, UNROLL), :]
        sources = es[pl.ds(base, UNROLL), :]
        counts = []
        for u in range(UNROLL):
            hot_t = jnp.where(sub == targets[u : u + 1, :], 1.0, 0.0).astype(BF16)
            hot_s = jnp.where(sub == sources[u : u + 1, :], 1.0, 0.0).astype(BF16)
            fwd = lax.dot_general(hot_t, hot_s, LANES, preferred_element_type=F32)
            bwd = lax.dot_general(hot_s, hot_t, LANES, preferred_element_type=F32)
            fwd_adj[base + u] = fwd.astype(BF16)
            bwd_adj[base + u] = bwd.astype(BF16)
            counts.append(jnp.sum(bwd, axis=0, keepdims=True))
        slot_counts[pl.ds(base, UNROLL), :] = jnp.concatenate(counts, axis=0)
        return 0

    lax.fori_loop(0, slots // UNROLL, build, 0)

    for d in reversed(q_far):
        arrive([x_copies[d]])
        block = xb.at[k * n_q + lax.rem(q + n_q - d, n_q)]
        x_core.append(send(block, block, sibling))

    tile_sub = lax.broadcasted_iota(jnp.int32, (n_y * 8, TILE), 0)
    wanted = (tile_sub // 8) * n_z + tile_sub % 8
    hits = (jnp.broadcast_to(trow[...], (n_y * 8, TILE)) == wanted) & (tile_sub % 8 < n_z)
    partial = jnp.dot(
        jnp.where(hits, 1.0, 0.0).astype(BF16),
        slot_counts[...].astype(BF16),
        preferred_element_type=F32,
    )
    deg[...] = partial.reshape(n_y, 8, TILE)
    deg_copies = [send(deg.at[lax.rem(y + d, n_y)], deg_r.at[d], at_y(d)) for d in y_far]
    self_term = jnp.dot(feat[...], ws[...], preferred_element_type=F32)

    meta_copy.wait()
    arrive(x_core)

    def forward(g, acc):
        for u in range(UNROLL):
            s = g * UNROLL + u
            word = meta_s[0, s]
            slot, col = word & 127, (word >> 7) & 31
            source = xb[(col & 1) * n_q + (col >> 1)]
            product = jnp.dot(fwd_adj[slot], source, preferred_element_type=F32)
            acc = jnp.where(word >= 4096, acc, 0.0) + product
            runs[s] = acc.astype(BF16)
        return acc

    lax.fori_loop(0, slots // UNROLL, forward, jnp.zeros((TILE, TILE), F32))

    def place_rows(i, _):
        word = meta_s[1, i]
        run = runs[word & 127]
        run = jnp.where(word >= 256, run, jnp.zeros_like(run))
        pa[i] = run[:HALF]
        pb[(i % n_z) * n_y + i // n_z] = run[HALF:]
        return 0

    lax.fori_loop(0, n_dst, place_rows, 0)

    a_copies = [
        send(pa.at[pl.ds(lax.rem(y + d, n_y) * n_z, n_z)], ra.at[d], at_y(d)) for d in y_far
    ]
    b_copies = [
        send(pb.at[pl.ds(lax.rem(z + d, n_z) * n_y, n_y)], rb.at[d], at_z(d)) for d in z_far
    ]

    arrive(deg_copies)
    summed = deg[y]
    for d in range(1, n_y):
        summed = summed + deg_r[d]
    deg2[...] = summed
    deg2_copies = [send(deg2, deg2_r.at[d], at_z(d)) for d in z_far]

    arrive(a_copies)
    total = pa[pl.ds(y * n_z, n_z)].astype(F32)
    for d in range(1, n_y):
        total = total + ra[d].astype(F32)
    sa[...] = total.astype(BF16)
    a2_copies = [send(sa.at[lax.rem(z + d, n_z)], ra2.at[d], at_z(d)) for d in z_far]

    arrive(deg2_copies)
    degree = deg2[...]
    for d in range(1, n_z):
        degree = degree + deg2_r[d]
    sub8 = lax.broadcasted_iota(jnp.int32, (8, TILE), 0)
    degree = jnp.sum(jnp.where(sub8 == z, degree, 0.0), axis=0, keepdims=True)
    inverse = 1.0 / (jnp.broadcast_to(degree, (TILE, TILE)).T + 1.0)

    arrive(b_copies)
    total = pb[pl.ds(z * n_y, n_y)].astype(F32)
    for d in range(1, n_z):
        total = total + rb[d].astype(F32)
    sb[...] = total.astype(BF16)
    b2_copies = [send(sb.at[lax.rem(y + d, n_y)], rb2.at[d], at_y(d)) for d in y_far]
    arrive(a2_copies)
    upper = sa[z].astype(F32)
    for d in range(1, n_z):
        upper = upper + ra2[d].astype(F32)
    arrive(b2_copies)
    lower = sb[y].astype(F32)
    for d in range(1, n_y):
        lower = lower + rb2[d].astype(F32)
    neighbour_sum = jnp.concatenate([upper, lower], axis=0)

    aggregate = (neighbour_sum * inverse).astype(BF16)
    preact = self_term + jnp.dot(aggregate, wn[...], preferred_element_type=F32) + bias[...]
    sigma = jax.nn.sigmoid(preact)
    grad_pre = (cot[...].astype(F32) * sigma * (1.0 + preact * (1.0 - sigma))).astype(BF16)
    scaled = lax.dot_general(grad_pre, wn[...], LANES, preferred_element_type=F32) * inverse
    scaled = scaled.astype(BF16)

    ga[y * n_z + z] = scaled[:HALF]
    gb[z * n_y + y] = scaled[HALF:]
    own_a, own_b = ga.at[y * n_z + z], gb.at[z * n_y + y]
    b_copies = [send(own_b, own_b, at_y(d)) for d in y_far]
    a_copies = [send(own_a, own_a, at_z(d)) for d in z_far]

    self_local = lax.dot_general(feat[...], grad_pre, ROWS, preferred_element_type=F32)
    neighbour_local = lax.dot_general(aggregate, grad_pre, ROWS, preferred_element_type=F32)
    bias_local = jnp.sum(grad_pre.astype(F32).reshape(TILE // 8, 8, TILE), axis=0)
    wl[0, :TILE] = self_local
    wl[1, :TILE] = neighbour_local
    wl[0, TILE:] = bias_local
    wl[1, TILE:] = bias_local
    w_core = send(wl.at[1 - k], wc, sibling)
    act_v[...] = (preact * sigma).astype(BF16)
    put(act_v, act_o)
    own_term = lax.dot_general(grad_pre, ws[...], LANES, preferred_element_type=F32)

    arrive([w_core])
    both = wl[k] + wc[...]
    for j in range(n_q):
        w1[j] = jnp.concatenate([both[j * wrows : (j + 1) * wrows], both[TILE:]], axis=0)
    wx_copies = [send(w1.at[lax.rem(q + d, n_q)], wx.at[d], at_q(d)) for d in q_far]

    arrive(a_copies)
    group_a = ga.at[pl.ds(y * n_z, n_z)]
    a_copies = [send(group_a, group_a, at_y(d)) for d in y_far]
    arrive(b_copies)
    group_b = gb.at[pl.ds(z * n_y, n_y)]
    b_copies = [send(group_b, group_b, at_z(d)) for d in z_far]

    arrive(wx_copies)
    summed = w1[q]
    for d in range(1, n_q):
        summed = summed + wx[d]
    w2[...] = summed
    wz_copies = [send(w2, wz.at[d], at_z(d)) for d in z_far]
    arrive(wz_copies)
    summed = w2[...]
    for d in range(1, n_z):
        summed = summed + wz[d]
    w3[...] = summed
    wy_copies = [send(w3, wy.at[d], at_y(d)) for d in y_far]

    arrive(a_copies)
    arrive(b_copies)

    def backward(g, acc):
        for u in range(UNROLL):
            s = g * UNROLL + u
            word = meta_s[2, s]
            slot, row = word & 127, (word >> 7) & 31
            target = jnp.concatenate([ga[row], gb[(row % n_z) * n_y + row // n_z]], axis=0)
            product = jnp.dot(bwd_adj[slot], target, preferred_element_type=F32)
            acc = jnp.where(word >= 4096, acc, 0.0) + product
            runs[s] = acc.astype(BF16)
        return acc

    lax.fori_loop(0, slots // UNROLL, backward, jnp.zeros((TILE, TILE), F32))

    def place_cols(j, _):
        word = meta_s[3, j]
        run = runs[word & 127]
        run = jnp.where(word >= 256, run, jnp.zeros_like(run))
        bp[(j % CORES) * n_q + j // CORES] = run
        return 0

    lax.fori_loop(0, n_src, place_cols, 0)

    b_core = {}
    for d in q_far + [0]:
        i = lax.rem(q + d, n_q)
        b_core[d] = send(bp.at[(1 - k) * n_q + i], br.at[i], sibling)
    arrive(wy_copies)
    summed = w3[...]
    for d in range(1, n_y):
        summed = summed + wy[d]
    summed = summed * scaling
    wo[k * n_q + q] = summed[:wrows]
    own_w = wo.at[k * n_q + q]
    wo_copies = {d: send(own_w, own_w, at_q(d)) for d in q_far}
    wo_core = [send(own_w, own_w, sibling)]
    bg_v[...] = jnp.sum(summed[wrows:], axis=0, keepdims=True)
    put(bg_v, bg_o)

    back_copies = []
    for d in q_far:
        i = lax.rem(q + d, n_q)
        arrive([b_core[d]])
        bs[i] = (bp[k * n_q + i].astype(F32) + br[i].astype(F32)).astype(BF16)
        back_copies.append(send(bs.at[i], br2.at[d], at_q(d)))
    arrive([b_core[0]])
    feature_grad = own_term + (bp[k * n_q + q].astype(F32) + br[q].astype(F32))

    for d in reversed(q_far):
        arrive([wo_copies[d]])
        block = wo.at[k * n_q + lax.rem(q + n_q - d, n_q)]
        wo_core.append(send(block, block, sibling))
    arrive(back_copies)
    for d in range(1, n_q):
        feature_grad = feature_grad + br2[d].astype(F32)
    fg_v[...] = feature_grad.astype(BF16)
    put(fg_v, fg_o)
    arrive(wo_core)
    put(wo.at[pl.ds(0, n_q)], sg_o)
    put(wo.at[pl.ds(n_q, n_q)], ng_o)
    for copy in local_out:
        copy.wait()
    for copy in started:
        copy.wait_send()


def hand_over(*refs):
    sources, results, sems = refs[:5], refs[5:10], refs[10]
    copies = [
        pltpu.make_async_copy(source, result, sems.at[i])
        for i, (source, result) in enumerate(zip(sources, results))
    ]
    for copy in copies:
        copy.start()
    for copy in copies:
        copy.wait()


def on_device(
    n_row,
    n_col,
    features,
    cotangent,
    self_weight,
    neighbour_weight,
    shift_bias,
    tile_rows,
    tile_cols,
    edge_targets,
    edge_sources,
):
    slots = edge_targets.shape[2]
    n_z = 4 if n_col >= 16 else 2
    n_y, n_q = n_col // n_z, n_row // CORES
    scaling = float((TILE * n_row * n_col) ** (-0.5))
    sizes = (n_q, n_y, n_z, slots, scaling)
    wrows = TILE // n_q
    n_dst, n_src = n_col, n_row
    copies = 6 * (n_y - 1) + 6 * (n_z - 1) + 4 * (n_q - 1) + 3 * n_q + 1
    scratch = [
        pltpu.VMEM((TILE, TILE), BF16),
        pltpu.VMEM((TILE, TILE), BF16),
        pltpu.VMEM((TILE, TILE), BF16),
        pltpu.VMEM((TILE, TILE), BF16),
        pltpu.VMEM((1, TILE), F32),
        pltpu.VMEM((1, slots), jnp.int32),
        pltpu.VMEM((1, slots), jnp.int32),
        pltpu.VMEM((slots, TILE), jnp.int32),
        pltpu.VMEM((slots, TILE), jnp.int32),
        pltpu.VMEM((TILE, TILE), BF16),
        pltpu.VMEM((TILE, TILE), BF16),
        pltpu.VMEM((1, TILE), F32),
        pltpu.VMEM((slots, TILE, TILE), BF16),
        pltpu.VMEM((slots, TILE, TILE), BF16),
        pltpu.VMEM((slots, TILE, TILE), BF16),
        pltpu.VMEM((slots, TILE), F32),
        pltpu.VMEM((8, TILE), jnp.int32),
        pltpu.SMEM((8, TILE), jnp.int32),
        pltpu.VMEM((n_src, TILE, TILE), BF16),
        pltpu.VMEM((n_dst, HALF, TILE), BF16),
        pltpu.VMEM((n_dst, HALF, TILE), BF16),
        pltpu.VMEM((n_y, n_z, HALF, TILE), BF16),
        pltpu.VMEM((n_z, n_y, HALF, TILE), BF16),
        pltpu.VMEM((n_z, HALF, TILE), BF16),
        pltpu.VMEM((n_y, HALF, TILE), BF16),
        pltpu.VMEM((n_z, HALF, TILE), BF16),
        pltpu.VMEM((n_y, HALF, TILE), BF16),
        pltpu.VMEM((n_y, 8, TILE), F32),
        pltpu.VMEM((n_y, 8, TILE), F32),
        pltpu.VMEM((8, TILE), F32),
        pltpu.VMEM((n_z, 8, TILE), F32),
        pltpu.VMEM((n_dst, HALF, TILE), BF16),
        pltpu.VMEM((n_dst, HALF, TILE), BF16),
        pltpu.VMEM((n_src, TILE, TILE), BF16),
        pltpu.VMEM((n_q, TILE, TILE), BF16),
        pltpu.VMEM((n_q, TILE, TILE), BF16),
        pltpu.VMEM((n_q, TILE, TILE), BF16),
        pltpu.VMEM((CORES, TILE + 8, TILE), F32),
        pltpu.VMEM((TILE + 8, TILE), F32),
        pltpu.VMEM((n_q, wrows + 8, TILE), F32),
        pltpu.VMEM((n_q, wrows + 8, TILE), F32),
        pltpu.VMEM((wrows + 8, TILE), F32),
        pltpu.VMEM((n_y, wrows + 8, TILE), F32),
        pltpu.VMEM((wrows + 8, TILE), F32),
        pltpu.VMEM((n_z, wrows + 8, TILE), F32),
        pltpu.VMEM((CORES * n_q, wrows, TILE), F32),
        pltpu.SemaphoreType.DMA((copies,)),
        pltpu.SemaphoreType.DMA((copies,)),
        pltpu.SemaphoreType.DMA,
        pltpu.SemaphoreType.DMA((10,)),
        pltpu.SemaphoreType.DMA((5,)),
    ]
    whole = pl.BlockSpec(memory_space=pl.ANY)
    out_shape = (
        jax.ShapeDtypeStruct((TILE, TILE), BF16),
        jax.ShapeDtypeStruct((TILE, TILE), BF16),
        jax.ShapeDtypeStruct((n_q, wrows, TILE), F32),
        jax.ShapeDtypeStruct((n_q, wrows, TILE), F32),
        jax.ShapeDtypeStruct((1, TILE), F32),
    )
    results = pl.pallas_call(
        functools.partial(layer_kernel, sizes),
        out_shape=out_shape,
        in_specs=[pl.BlockSpec(memory_space=pltpu.HBM)] * 9,
        out_specs=(whole,) * 5,
        scratch_shapes=scratch,
        compiler_params=pltpu.CompilerParams(
            collective_id=0, has_side_effects=True, vmem_limit_bytes=60 * 2**20
        ),
        name="sage_layer",
    )(
        features,
        cotangent,
        self_weight,
        neighbour_weight,
        shift_bias.reshape(1, TILE),
        tile_rows.reshape(1, slots),
        tile_cols.reshape(1, slots),
        edge_targets.reshape(slots, -1),
        edge_sources.reshape(slots, -1),
    )
    act, fg, sg, ng, bg = pl.pallas_call(
        hand_over,
        out_shape=out_shape,
        in_specs=[pl.BlockSpec(memory_space=pltpu.VMEM)] * 5,
        out_specs=(pl.BlockSpec(memory_space=pltpu.HBM),) * 5,
        scratch_shapes=[pltpu.SemaphoreType.DMA((5,))],
        name="hand_over",
    )(*results)
    return act, fg, sg.reshape(TILE, TILE), ng.reshape(TILE, TILE), bg.reshape(TILE)


def solution(mesh):
    in_specs = (
        P(("row", "col"), None),
        P(("row", "col"), None),
        P(),
        P(),
        P(),
        P("row", "col", None),
        P("row", "col", None),
        P("row", "col", None, None),
        P("row", "col", None, None),
    )
    out_specs = (P(("row", "col"), None), P(("row", "col"), None), P(), P(), P())
    body = functools.partial(on_device, mesh.shape["row"], mesh.shape["col"])
    return jax.shard_map(
        body, mesh=mesh, in_specs=in_specs, out_specs=out_specs, check_vma=False
    )
```

```python
import functools

import jax
import jax.numpy as jnp
from jax import lax
from jax.experimental import pallas as pl
from jax.experimental.pallas import tpu as pltpu
from jax.sharding import PartitionSpec as P

TILE = 128
HALF = TILE // 2
CORES = 2
UNROLL = 16
MESH = pl.DeviceIdType.MESH
F32 = jnp.float32
BF16 = jnp.bfloat16
LANES = (((1,), (1,)), ((), ()))
ROWS = (((0,), (0,)), ((), ()))


def far_first(n):
    return sorted(range(1, n), key=lambda d: -min(d, n - d))


def layer_kernel(
    sizes,
    feat_h,
    cot_h,
    ws_h,
    wn_h,
    bias_h,
    trow_h,
    tcol_h,
    et_h,
    es_h,
    act_o,
    fg_o,
    sg_o,
    ng_o,
    bg_o,
    feat,
    cot,
    ws,
    wn,
    bias,
    trow,
    tcol,
    et,
    es,
    fwd_adj,
    bwd_adj,
    runs,
    slot_counts,
    meta_v,
    meta_s,
    xb,
    pa,
    pb,
    ra,
    rb,
    sa,
    sb,
    ra2,
    rb2,
    deg,
    deg_r,
    deg2,
    deg2_r,
    ga,
    gb,
    bp,
    br,
    bs,
    br2,
    wl,
    wc,
    w1,
    wx,
    w2,
    wy,
    w3,
    wz,
    wo,
    send_sems,
    recv_sems,
    meta_sem,
    in_sems,
):
    n_q, n_y, n_z, slots, scaling = sizes
    r = lax.axis_index("row")
    c = lax.axis_index("col")
    q, k = r // CORES, r % CORES
    y, z = c // n_z, c % n_z
    n_src = n_q * CORES
    n_dst = n_y * n_z
    wrows = TILE // n_y

    def at_y(d):
        return (r, lax.rem(y + d, n_y) * n_z + z)

    def at_z(d):
        return (r, y * n_z + lax.rem(z + d, n_z))

    def at_q(d):
        return (lax.rem(q + d, n_q) * CORES + k, c)

    sibling = (q * CORES + 1 - k, c)

    used = [0]
    started = []

    def send(src, dst, device):
        i = used[0]
        used[0] += 1
        copy = pltpu.make_async_remote_copy(
            src_ref=src,
            dst_ref=dst,
            send_sem=send_sems.at[i],
            recv_sem=recv_sems.at[i],
            device_id=device,
            device_id_type=MESH,
        )
        copy.start()
        started.append(copy)
        return copy

    def arrive(copies):
        for copy in copies:
            copy.wait_recv()

    y_far, z_far, q_far = far_first(n_y), far_first(n_z), far_first(n_q)

    barrier = pltpu.get_barrier_semaphore()
    partners = [at_q(d) for d in q_far] + [at_y(d) for d in y_far]
    partners += [at_z(d) for d in z_far] + [sibling]
    for partner in partners:
        pl.semaphore_signal(barrier, inc=1, device_id=partner, device_id_type=MESH)

    local_in = []
    for i, (far, near) in enumerate(
        zip(
            (feat_h, trow_h, tcol_h, et_h, es_h, feat_h, ws_h, wn_h, bias_h, cot_h),
            (xb.at[k * n_q + q], trow, tcol, et, es, feat, ws, wn, bias, cot),
        )
    ):
        local_in.append(pltpu.make_async_copy(far, near, in_sems.at[i]))
        local_in[-1].start()

    pl.semaphore_wait(barrier, len(partners))

    mine = xb.at[k * n_q + q]
    x_copies = {d: send(feat_h, mine, at_q(d)) for d in q_far}
    x_core = [send(feat_h, mine, sibling)]
    for copy in local_in:
        copy.wait()

    sub = lax.broadcasted_iota(jnp.int32, (TILE, TILE), 0)
    lane = lax.broadcasted_iota(jnp.int32, (TILE, TILE), 1)
    rows_l = jnp.broadcast_to(trow[...], (TILE, TILE))
    cols_l = jnp.broadcast_to(tcol[...], (TILE, TILE))
    rows_s, cols_s = rows_l.T, cols_l.T

    def order(ids_l, ids_s, other_s):
        before = (ids_l < ids_s) | ((ids_l == ids_s) & (lane < sub))
        rank = jnp.sum(before.astype(jnp.int32), axis=1, keepdims=True)
        same = jnp.sum(((ids_l == ids_s) & (lane < sub)).astype(jnp.int32), axis=1, keepdims=True)
        packed = sub + other_s * 128 + jnp.minimum(same, 1) * 4096
        ordered = jnp.sum(jnp.where(rank == lane, packed, 0), axis=0, keepdims=True)
        upto = jnp.sum((ids_s <= lane).astype(jnp.int32), axis=0, keepdims=True)
        below = jnp.sum((ids_s < lane).astype(jnp.int32), axis=0, keepdims=True)
        ends = jnp.maximum(upto - 1, 0) + jnp.where(upto > below, 256, 0)
        return ordered, ends

    by_row, row_ends = order(rows_l, rows_s, cols_s)
    by_col, col_ends = order(cols_l, cols_s, rows_s)
    zero_row = jnp.zeros_like(by_row)
    meta_v[...] = jnp.concatenate([by_row, row_ends, by_col, col_ends] + [zero_row] * 4, axis=0)
    meta_copy = pltpu.make_async_copy(meta_v, meta_s, meta_sem)
    meta_copy.start()


    def build(g, _):
        base = pl.multiple_of(g * UNROLL, UNROLL)
        targets = et[pl.ds(base, UNROLL), :]
        sources = es[pl.ds(base, UNROLL), :]
        counts = []
        for u in range(UNROLL):
            hot_t = jnp.where(sub == targets[u : u + 1, :], 1.0, 0.0).astype(BF16)
            hot_s = jnp.where(sub == sources[u : u + 1, :], 1.0, 0.0).astype(BF16)
            fwd = lax.dot_general(hot_t, hot_s, LANES, preferred_element_type=F32)
            bwd = lax.dot_general(hot_s, hot_t, LANES, preferred_element_type=F32)
            fwd_adj[base + u] = fwd.astype(BF16)
            bwd_adj[base + u] = bwd.astype(BF16)
            counts.append(jnp.sum(bwd, axis=0, keepdims=True))
        slot_counts[pl.ds(base, UNROLL), :] = jnp.concatenate(counts, axis=0)
        return 0

    lax.fori_loop(0, slots // UNROLL, build, 0)

    for d in reversed(q_far):
        arrive([x_copies[d]])
        block = xb.at[k * n_q + lax.rem(q + n_q - d, n_q)]
        x_core.append(send(block, block, sibling))

    tile_sub = lax.broadcasted_iota(jnp.int32, (n_y * 8, TILE), 0)
    wanted = (tile_sub // 8) * n_z + tile_sub % 8
    hits = (jnp.broadcast_to(trow[...], (n_y * 8, TILE)) == wanted) & (tile_sub % 8 < n_z)
    partial = jnp.dot(
        jnp.where(hits, 1.0, 0.0).astype(BF16),
        slot_counts[...].astype(BF16),
        preferred_element_type=F32,
    )
    deg[...] = partial.reshape(n_y, 8, TILE)
    deg_copies = [send(deg.at[lax.rem(y + d, n_y)], deg_r.at[d], at_y(d)) for d in y_far]
    self_term = jnp.dot(feat[...], ws[...], preferred_element_type=F32)

    meta_copy.wait()
    arrive(x_core)

    def forward(g, acc):
        for u in range(UNROLL):
            s = g * UNROLL + u
            word = meta_s[0, s]
            slot, col = word & 127, (word >> 7) & 31
            source = xb[(col & 1) * n_q + (col >> 1)]
            product = jnp.dot(fwd_adj[slot], source, preferred_element_type=F32)
            acc = jnp.where(word >= 4096, acc, 0.0) + product
            runs[s] = acc.astype(BF16)
        return acc

    lax.fori_loop(0, slots // UNROLL, forward, jnp.zeros((TILE, TILE), F32))

    def place_rows(i, _):
        word = meta_s[1, i]
        run = runs[word & 127]
        run = jnp.where(word >= 256, run, jnp.zeros_like(run))
        pa[i] = run[:HALF]
        pb[(i % n_z) * n_y + i // n_z] = run[HALF:]
        return 0

    lax.fori_loop(0, n_dst, place_rows, 0)

    a_copies = [
        send(pa.at[pl.ds(lax.rem(y + d, n_y) * n_z, n_z)], ra.at[d], at_y(d)) for d in y_far
    ]
    b_copies = [
        send(pb.at[pl.ds(lax.rem(z + d, n_z) * n_y, n_y)], rb.at[d], at_z(d)) for d in z_far
    ]

    arrive(deg_copies)
    summed = deg[y]
    for d in range(1, n_y):
        summed = summed + deg_r[d]
    deg2[...] = summed
    deg2_copies = [send(deg2, deg2_r.at[d], at_z(d)) for d in z_far]

    arrive(a_copies)
    total = pa[pl.ds(y * n_z, n_z)].astype(F32)
    for d in range(1, n_y):
        total = total + ra[d].astype(F32)
    sa[...] = total.astype(BF16)
    a2_copies = [send(sa.at[lax.rem(z + d, n_z)], ra2.at[d], at_z(d)) for d in z_far]

    arrive(deg2_copies)
    degree = deg2[...]
    for d in range(1, n_z):
        degree = degree + deg2_r[d]
    sub8 = lax.broadcasted_iota(jnp.int32, (8, TILE), 0)
    degree = jnp.sum(jnp.where(sub8 == z, degree, 0.0), axis=0, keepdims=True)
    inverse = 1.0 / (jnp.broadcast_to(degree, (TILE, TILE)).T + 1.0)

    arrive(b_copies)
    total = pb[pl.ds(z * n_y, n_y)].astype(F32)
    for d in range(1, n_z):
        total = total + rb[d].astype(F32)
    sb[...] = total.astype(BF16)
    b2_copies = [send(sb.at[lax.rem(y + d, n_y)], rb2.at[d], at_y(d)) for d in y_far]
    arrive(a2_copies)
    upper = sa[z].astype(F32)
    for d in range(1, n_z):
        upper = upper + ra2[d].astype(F32)
    arrive(b2_copies)
    lower = sb[y].astype(F32)
    for d in range(1, n_y):
        lower = lower + rb2[d].astype(F32)
    neighbour_sum = jnp.concatenate([upper, lower], axis=0)

    aggregate = (neighbour_sum * inverse).astype(BF16)
    preact = self_term + jnp.dot(aggregate, wn[...], preferred_element_type=F32) + bias[...]
    sigma = jax.nn.sigmoid(preact)
    grad_pre = (cot[...].astype(F32) * sigma * (1.0 + preact * (1.0 - sigma))).astype(BF16)
    scaled = lax.dot_general(grad_pre, wn[...], LANES, preferred_element_type=F32) * inverse
    scaled = scaled.astype(BF16)

    ga[y * n_z + z] = scaled[:HALF]
    gb[z * n_y + y] = scaled[HALF:]
    own_a, own_b = ga.at[y * n_z + z], gb.at[z * n_y + y]
    b_copies = [send(own_b, own_b, at_y(d)) for d in y_far]
    a_copies = [send(own_a, own_a, at_z(d)) for d in z_far]

    self_local = lax.dot_general(feat[...], grad_pre, ROWS, preferred_element_type=F32)
    neighbour_local = lax.dot_general(aggregate, grad_pre, ROWS, preferred_element_type=F32)
    bias_local = jnp.sum(grad_pre.astype(F32).reshape(TILE // 8, 8, TILE), axis=0)
    wl[0, :TILE] = self_local
    wl[1, :TILE] = neighbour_local
    wl[0, TILE:] = bias_local
    wl[1, TILE:] = bias_local
    w_core = send(wl.at[1 - k], wc, sibling)
    act_o[...] = (preact * sigma).astype(BF16)
    own_term = lax.dot_general(grad_pre, ws[...], LANES, preferred_element_type=F32)

    arrive([w_core])
    both = wl[k] + wc[...]
    for j in range(n_y):
        w1[j] = jnp.concatenate([both[j * wrows : (j + 1) * wrows], both[TILE:]], axis=0)
    wy_copies = [send(w1.at[lax.rem(y + d, n_y)], wy.at[d], at_y(d)) for d in y_far]

    arrive(a_copies)
    group_a = ga.at[pl.ds(y * n_z, n_z)]
    a_copies = [send(group_a, group_a, at_y(d)) for d in y_far]
    arrive(b_copies)
    group_b = gb.at[pl.ds(z * n_y, n_y)]
    b_copies = [send(group_b, group_b, at_z(d)) for d in z_far]

    arrive(wy_copies)
    summed = w1[y]
    for d in range(1, n_y):
        summed = summed + wy[d]
    w2[...] = summed
    wz_copies = [send(w2, wz.at[d], at_z(d)) for d in z_far]
    arrive(wz_copies)
    summed = w2[...]
    for d in range(1, n_z):
        summed = summed + wz[d]
    w3[...] = summed
    wx_copies = [send(w3, wx.at[d], at_q(d)) for d in q_far]

    arrive(a_copies)
    arrive(b_copies)

    def backward(g, acc):
        for u in range(UNROLL):
            s = g * UNROLL + u
            word = meta_s[2, s]
            slot, row = word & 127, (word >> 7) & 31
            target = jnp.concatenate([ga[row], gb[(row % n_z) * n_y + row // n_z]], axis=0)
            product = jnp.dot(bwd_adj[slot], target, preferred_element_type=F32)
            acc = jnp.where(word >= 4096, acc, 0.0) + product
            runs[s] = acc.astype(BF16)
        return acc

    lax.fori_loop(0, slots // UNROLL, backward, jnp.zeros((TILE, TILE), F32))

    def place_cols(j, _):
        word = meta_s[3, j]
        run = runs[word & 127]
        run = jnp.where(word >= 256, run, jnp.zeros_like(run))
        bp[(j % CORES) * n_q + j // CORES] = run
        return 0

    lax.fori_loop(0, n_src, place_cols, 0)

    b_core = {}
    for d in q_far + [0]:
        i = lax.rem(q + d, n_q)
        b_core[d] = send(bp.at[(1 - k) * n_q + i], br.at[i], sibling)
    back_copies = []
    for d in q_far:
        i = lax.rem(q + d, n_q)
        arrive([b_core[d]])
        bs[i] = (bp[k * n_q + i].astype(F32) + br[i].astype(F32)).astype(BF16)
        back_copies.append(send(bs.at[i], br2.at[d], at_q(d)))
    arrive([b_core[0]])
    feature_grad = own_term + (bp[k * n_q + q].astype(F32) + br[q].astype(F32))

    arrive(wx_copies)
    summed = w3[...]
    for d in range(1, n_q):
        summed = summed + wx[d]
    summed = summed * scaling
    wo[k * n_y + y] = summed[:wrows]
    own_w = wo.at[k * n_y + y]
    wo_copies = {d: send(own_w, own_w, at_y(d)) for d in y_far}
    wo_core = [send(own_w, own_w, sibling)]
    bg_o[...] = jnp.sum(summed[wrows:], axis=0, keepdims=True)

    for d in reversed(y_far):
        arrive([wo_copies[d]])
        block = wo.at[k * n_y + lax.rem(y + n_y - d, n_y)]
        wo_core.append(send(block, block, sibling))
    arrive(back_copies)
    for d in range(1, n_q):
        feature_grad = feature_grad + br2[d].astype(F32)
    fg_o[...] = feature_grad.astype(BF16)
    arrive(wo_core)
    sg_o[...] = wo[pl.ds(0, n_y)]
    ng_o[...] = wo[pl.ds(n_y, n_y)]
    for copy in started:
        copy.wait_send()


def hand_over(*refs):
    sources, results, sems = refs[:5], refs[5:10], refs[10]
    copies = [
        pltpu.make_async_copy(source, result, sems.at[i])
        for i, (source, result) in enumerate(zip(sources, results))
    ]
    for copy in copies:
        copy.start()
    for copy in copies:
        copy.wait()


def on_device(
    n_row,
    n_col,
    features,
    cotangent,
    self_weight,
    neighbour_weight,
    shift_bias,
    tile_rows,
    tile_cols,
    edge_targets,
    edge_sources,
):
    slots = edge_targets.shape[2]
    n_z = 4 if n_col >= 16 else 2
    n_y, n_q = n_col // n_z, n_row // CORES
    scaling = float((TILE * n_row * n_col) ** (-0.5))
    sizes = (n_q, n_y, n_z, slots, scaling)
    wrows = TILE // n_y
    n_dst, n_src = n_col, n_row
    copies = 7 * (n_y - 1) + 6 * (n_z - 1) + 3 * (n_q - 1) + 2 * n_q + n_y + 1
    scratch = [
        pltpu.VMEM((TILE, TILE), BF16),
        pltpu.VMEM((TILE, TILE), BF16),
        pltpu.VMEM((TILE, TILE), BF16),
        pltpu.VMEM((TILE, TILE), BF16),
        pltpu.VMEM((1, TILE), F32),
        pltpu.VMEM((1, slots), jnp.int32),
        pltpu.VMEM((1, slots), jnp.int32),
        pltpu.VMEM((slots, TILE), jnp.int32),
        pltpu.VMEM((slots, TILE), jnp.int32),
        pltpu.VMEM((slots, TILE, TILE), BF16),
        pltpu.VMEM((slots, TILE, TILE), BF16),
        pltpu.VMEM((slots, TILE, TILE), BF16),
        pltpu.VMEM((slots, TILE), F32),
        pltpu.VMEM((8, TILE), jnp.int32),
        pltpu.SMEM((8, TILE), jnp.int32),
        pltpu.VMEM((n_src, TILE, TILE), BF16),
        pltpu.VMEM((n_dst, HALF, TILE), BF16),
        pltpu.VMEM((n_dst, HALF, TILE), BF16),
        pltpu.VMEM((n_y, n_z, HALF, TILE), BF16),
        pltpu.VMEM((n_z, n_y, HALF, TILE), BF16),
        pltpu.VMEM((n_z, HALF, TILE), BF16),
        pltpu.VMEM((n_y, HALF, TILE), BF16),
        pltpu.VMEM((n_z, HALF, TILE), BF16),
        pltpu.VMEM((n_y, HALF, TILE), BF16),
        pltpu.VMEM((n_y, 8, TILE), F32),
        pltpu.VMEM((n_y, 8, TILE), F32),
        pltpu.VMEM((8, TILE), F32),
        pltpu.VMEM((n_z, 8, TILE), F32),
        pltpu.VMEM((n_dst, HALF, TILE), BF16),
        pltpu.VMEM((n_dst, HALF, TILE), BF16),
        pltpu.VMEM((n_src, TILE, TILE), BF16),
        pltpu.VMEM((n_q, TILE, TILE), BF16),
        pltpu.VMEM((n_q, TILE, TILE), BF16),
        pltpu.VMEM((n_q, TILE, TILE), BF16),
        pltpu.VMEM((CORES, TILE + 8, TILE), F32),
        pltpu.VMEM((TILE + 8, TILE), F32),
        pltpu.VMEM((n_y, wrows + 8, TILE), F32),
        pltpu.VMEM((n_q, wrows + 8, TILE), F32),
        pltpu.VMEM((wrows + 8, TILE), F32),
        pltpu.VMEM((n_y, wrows + 8, TILE), F32),
        pltpu.VMEM((wrows + 8, TILE), F32),
        pltpu.VMEM((n_z, wrows + 8, TILE), F32),
        pltpu.VMEM((CORES * n_y, wrows, TILE), F32),
        pltpu.SemaphoreType.DMA((copies,)),
        pltpu.SemaphoreType.DMA((copies,)),
        pltpu.SemaphoreType.DMA,
        pltpu.SemaphoreType.DMA((10,)),
    ]
    out_shape = (
        jax.ShapeDtypeStruct((TILE, TILE), BF16),
        jax.ShapeDtypeStruct((TILE, TILE), BF16),
        jax.ShapeDtypeStruct((n_y, wrows, TILE), F32),
        jax.ShapeDtypeStruct((n_y, wrows, TILE), F32),
        jax.ShapeDtypeStruct((1, TILE), F32),
    )
    operands = (
        features,
        cotangent,
        self_weight,
        neighbour_weight,
        shift_bias.reshape(1, TILE),
        tile_rows.reshape(1, slots),
        tile_cols.reshape(1, slots),
        edge_targets.reshape(slots, -1),
        edge_sources.reshape(slots, -1),
    )
    operands = [pltpu.with_memory_space_constraint(v, pltpu.HBM) for v in operands]
    results = pl.pallas_call(
        functools.partial(layer_kernel, sizes),
        out_shape=out_shape,
        in_specs=[pl.BlockSpec(memory_space=pltpu.HBM)] * 9,
        out_specs=(pl.BlockSpec(memory_space=pltpu.VMEM),) * 5,
        scratch_shapes=scratch,
        compiler_params=pltpu.CompilerParams(
            collective_id=0, has_side_effects=True, vmem_limit_bytes=44 * 2**20
        ),
        name="sage_layer",
    )(*operands)
    act, fg, sg, ng, bg = pl.pallas_call(
        hand_over,
        out_shape=out_shape,
        in_specs=[pl.BlockSpec(memory_space=pltpu.VMEM)] * 5,
        out_specs=(pl.BlockSpec(memory_space=pltpu.HBM),) * 5,
        scratch_shapes=[pltpu.SemaphoreType.DMA((5,))],
        compiler_params=pltpu.CompilerParams(vmem_limit_bytes=2 * 2**20),
        name="hand_over",
    )(*results)
    return act, fg, sg.reshape(TILE, TILE), ng.reshape(TILE, TILE), bg.reshape(TILE)


def solution(mesh):
    in_specs = (
        P(("row", "col"), None),
        P(("row", "col"), None),
        P(),
        P(),
        P(),
        P("row", "col", None),
        P("row", "col", None),
        P("row", "col", None, None),
        P("row", "col", None, None),
    )
    out_specs = (P(("row", "col"), None), P(("row", "col"), None), P(), P(), P())
    body = functools.partial(on_device, mesh.shape["row"], mesh.shape["col"])
    return jax.shard_map(
        body, mesh=mesh, in_specs=in_specs, out_specs=out_specs, check_vma=False
    )
```

```python
import functools

import jax
import jax.numpy as jnp
from jax import lax
from jax.experimental import pallas as pl
from jax.experimental.pallas import tpu as pltpu
from jax.sharding import PartitionSpec as P

TILE = 128
HALF = TILE // 2
CORES = 2
UNROLL = 16
STRETCH = 64
MESH = pl.DeviceIdType.MESH
F32 = jnp.float32
BF16 = jnp.bfloat16
LANES = (((1,), (1,)), ((), ()))
ROWS = (((0,), (0,)), ((), ()))


def far_first(n):
    return sorted(range(1, n), key=lambda d: -min(d, n - d))


def layer_kernel(
    sizes,
    feat_h,
    cot_h,
    ws_h,
    wn_h,
    bias_h,
    trow_h,
    tcol_h,
    et_h,
    es_h,
    act_o,
    fg_o,
    sg_o,
    ng_o,
    bg_o,
    feat,
    cot,
    ws,
    wn,
    bias,
    trow,
    tcol,
    et,
    es,
    fwd_adj,
    bwd_adj,
    runs,
    slot_counts,
    meta_v,
    meta_s,
    xb,
    pa,
    pb,
    ra,
    rb,
    sa,
    sb,
    ra2,
    rb2,
    deg,
    deg_r,
    deg2,
    deg2_r,
    ga,
    gb,
    bp,
    br,
    bs,
    br2,
    wl,
    wc,
    w1,
    wx,
    w2,
    wy,
    w3,
    wz,
    wo,
    send_sems,
    recv_sems,
    meta_sem,
    in_sems,
):
    n_q, n_y, n_z, slots, scaling = sizes
    r = lax.axis_index("row")
    c = lax.axis_index("col")
    q, k = r // CORES, r % CORES
    y, z = c // n_z, c % n_z
    n_src = n_q * CORES
    n_dst = n_y * n_z
    wrows = TILE // n_y

    def at_y(d):
        return (r, lax.rem(y + d, n_y) * n_z + z)

    def at_z(d):
        return (r, y * n_z + lax.rem(z + d, n_z))

    n_x = n_q // 2
    x, h = q // 2, q % 2
    q_steps = [(dx, dh) for dx in range(n_x) for dh in range(2)]

    def q_to(d):
        return lax.rem(x + q_steps[d][0], n_x) * 2 + lax.rem(h + q_steps[d][1], 2)

    def q_from(d):
        return lax.rem(x + n_x - q_steps[d][0], n_x) * 2 + lax.rem(h + q_steps[d][1], 2)

    def at_q(d):
        return (q_to(d) * CORES + k, c)

    sibling = (q * CORES + 1 - k, c)

    used = [0]
    started = []

    def send(src, dst, device):
        i = used[0]
        used[0] += 1
        copy = pltpu.make_async_remote_copy(
            src_ref=src,
            dst_ref=dst,
            send_sem=send_sems.at[i],
            recv_sem=recv_sems.at[i],
            device_id=device,
            device_id_type=MESH,
        )
        copy.start()
        started.append(copy)
        return copy

    def arrive(copies):
        for copy in copies:
            copy.wait_recv()

    y_far, z_far = far_first(n_y), far_first(n_z)
    q_far = sorted(
        range(1, n_q),
        key=lambda d: -min(q_steps[d][0], n_x - q_steps[d][0]) - 4 * q_steps[d][1],
    )

    barrier = pltpu.get_barrier_semaphore()
    partners = [at_q(d) for d in q_far] + [at_y(d) for d in y_far]
    partners += [at_z(d) for d in z_far] + [sibling]
    for partner in partners:
        pl.semaphore_signal(barrier, inc=1, device_id=partner, device_id_type=MESH)

    local_in = []
    for i, (far, near) in enumerate(
        zip(
            (feat_h, trow_h, tcol_h, et_h, es_h, feat_h, ws_h, wn_h, bias_h, cot_h),
            (xb.at[k * n_q + q], trow, tcol, et, es, feat, ws, wn, bias, cot),
        )
    ):
        local_in.append(pltpu.make_async_copy(far, near, in_sems.at[i]))
        local_in[-1].start()

    pl.semaphore_wait(barrier, len(partners))

    mine = xb.at[k * n_q + q]
    x_copies = {d: send(feat_h, mine, at_q(d)) for d in q_far}
    x_core = [send(feat_h, mine, sibling)]
    for copy in local_in:
        copy.wait()

    sub = lax.broadcasted_iota(jnp.int32, (TILE, TILE), 0)
    lane = lax.broadcasted_iota(jnp.int32, (TILE, TILE), 1)
    rows_l = jnp.broadcast_to(trow[...], (TILE, TILE))
    cols_l = jnp.broadcast_to(tcol[...], (TILE, TILE))
    rows_s, cols_s = rows_l.T, cols_l.T

    def order(ids_l, ids_s, other_s):
        before = (ids_l < ids_s) | ((ids_l == ids_s) & (lane < sub))
        rank = jnp.sum(before.astype(jnp.int32), axis=1, keepdims=True)
        same = jnp.sum(((ids_l == ids_s) & (lane < sub)).astype(jnp.int32), axis=1, keepdims=True)
        packed = sub + other_s * 128 + jnp.minimum(same, 1) * 4096
        ordered = jnp.sum(jnp.where(rank == lane, packed, 0), axis=0, keepdims=True)
        upto = jnp.sum((ids_s <= lane).astype(jnp.int32), axis=0, keepdims=True)
        below = jnp.sum((ids_s < lane).astype(jnp.int32), axis=0, keepdims=True)
        ends = jnp.maximum(upto - 1, 0) + jnp.where(upto > below, 256, 0)
        return ordered, ends

    by_row, row_ends = order(rows_l, rows_s, cols_s)
    by_col, col_ends = order(cols_l, cols_s, rows_s)
    zero_row = jnp.zeros_like(by_row)
    meta_v[...] = jnp.concatenate([by_row, row_ends, by_col, col_ends] + [zero_row] * 4, axis=0)
    meta_copy = pltpu.make_async_copy(meta_v, meta_s, meta_sem)
    meta_copy.start()


    def build(g, _):
        base = pl.multiple_of(g * UNROLL, UNROLL)
        targets = et[pl.ds(base, UNROLL), :]
        sources = es[pl.ds(base, UNROLL), :]
        counts = []
        for u in range(UNROLL):
            hot_t = jnp.where(sub == targets[u : u + 1, :], 1.0, 0.0).astype(BF16)
            hot_s = jnp.where(sub == sources[u : u + 1, :], 1.0, 0.0).astype(BF16)
            fwd = lax.dot_general(hot_t, hot_s, LANES, preferred_element_type=F32)
            bwd = lax.dot_general(hot_s, hot_t, LANES, preferred_element_type=F32)
            fwd_adj[base + u] = fwd.astype(BF16)
            bwd_adj[base + u] = bwd.astype(BF16)
            counts.append(jnp.sum(bwd, axis=0, keepdims=True))
        slot_counts[pl.ds(base, UNROLL), :] = jnp.concatenate(counts, axis=0)
        return 0

    lax.fori_loop(0, slots // UNROLL, build, 0)

    for d in reversed(q_far):
        arrive([x_copies[d]])
        block = xb.at[k * n_q + q_from(d)]
        x_core.append(send(block, block, sibling))

    tile_sub = lax.broadcasted_iota(jnp.int32, (n_y * 8, TILE), 0)
    wanted = (tile_sub // 8) * n_z + tile_sub % 8
    hits = (jnp.broadcast_to(trow[...], (n_y * 8, TILE)) == wanted) & (tile_sub % 8 < n_z)
    partial = jnp.dot(
        jnp.where(hits, 1.0, 0.0).astype(BF16),
        slot_counts[...].astype(BF16),
        preferred_element_type=F32,
    )
    deg[...] = partial.reshape(n_y, 8, TILE)
    deg_copies = [send(deg.at[lax.rem(y + d, n_y)], deg_r.at[d], at_y(d)) for d in y_far]
    self_term = jnp.dot(feat[...], ws[...], preferred_element_type=F32)

    meta_copy.wait()
    arrive(x_core)

    def forward(g, acc):
        for u in range(STRETCH):
            s = g * STRETCH + u
            word = meta_s[0, s]
            slot, col = word & 127, (word >> 7) & 31
            source = xb[(col & 1) * n_q + (col >> 1)]
            product = jnp.dot(fwd_adj[slot], source, preferred_element_type=F32)
            acc = jnp.where(word >= 4096, acc, 0.0) + product
            runs[s] = acc.astype(BF16)
        return acc

    lax.fori_loop(0, slots // STRETCH, forward, jnp.zeros((TILE, TILE), F32))

    def place_rows(i, _):
        word = meta_s[1, i]
        run = runs[word & 127]
        run = jnp.where(word >= 256, run, jnp.zeros_like(run))
        pa[i] = run[:HALF]
        pb[(i % n_z) * n_y + i // n_z] = run[HALF:]
        return 0

    lax.fori_loop(0, n_dst, place_rows, 0)

    a_copies = [
        send(pa.at[pl.ds(lax.rem(y + d, n_y) * n_z, n_z)], ra.at[d], at_y(d)) for d in y_far
    ]
    b_copies = [
        send(pb.at[pl.ds(lax.rem(z + d, n_z) * n_y, n_y)], rb.at[d], at_z(d)) for d in z_far
    ]

    arrive(deg_copies)
    summed = deg[y]
    for d in range(1, n_y):
        summed = summed + deg_r[d]
    deg2[...] = summed
    deg2_copies = [send(deg2, deg2_r.at[d], at_z(d)) for d in z_far]

    arrive(a_copies)
    total = pa[pl.ds(y * n_z, n_z)].astype(F32)
    for d in range(1, n_y):
        total = total + ra[d].astype(F32)
    sa[...] = total.astype(BF16)
    a2_copies = [send(sa.at[lax.rem(z + d, n_z)], ra2.at[d], at_z(d)) for d in z_far]

    arrive(deg2_copies)
    degree = deg2[...]
    for d in range(1, n_z):
        degree = degree + deg2_r[d]
    sub8 = lax.broadcasted_iota(jnp.int32, (8, TILE), 0)
    degree = jnp.sum(jnp.where(sub8 == z, degree, 0.0), axis=0, keepdims=True)
    inverse = 1.0 / (jnp.broadcast_to(degree, (TILE, TILE)).T + 1.0)

    arrive(b_copies)
    total = pb[pl.ds(z * n_y, n_y)].astype(F32)
    for d in range(1, n_z):
        total = total + rb[d].astype(F32)
    sb[...] = total.astype(BF16)
    b2_copies = [send(sb.at[lax.rem(y + d, n_y)], rb2.at[d], at_y(d)) for d in y_far]
    arrive(a2_copies)
    upper = sa[z].astype(F32)
    for d in range(1, n_z):
        upper = upper + ra2[d].astype(F32)
    arrive(b2_copies)
    lower = sb[y].astype(F32)
    for d in range(1, n_y):
        lower = lower + rb2[d].astype(F32)
    neighbour_sum = jnp.concatenate([upper, lower], axis=0)

    aggregate = (neighbour_sum * inverse).astype(BF16)
    preact = self_term + jnp.dot(aggregate, wn[...], preferred_element_type=F32) + bias[...]
    sigma = jax.nn.sigmoid(preact)
    grad_pre = (cot[...].astype(F32) * sigma * (1.0 + preact * (1.0 - sigma))).astype(BF16)
    scaled = lax.dot_general(grad_pre, wn[...], LANES, preferred_element_type=F32) * inverse
    scaled = scaled.astype(BF16)

    ga[y * n_z + z] = scaled[:HALF]
    gb[z * n_y + y] = scaled[HALF:]
    own_a, own_b = ga.at[y * n_z + z], gb.at[z * n_y + y]
    b_copies = [send(own_b, own_b, at_y(d)) for d in y_far]
    a_copies = [send(own_a, own_a, at_z(d)) for d in z_far]

    self_local = lax.dot_general(feat[...], grad_pre, ROWS, preferred_element_type=F32)
    neighbour_local = lax.dot_general(aggregate, grad_pre, ROWS, preferred_element_type=F32)
    bias_local = jnp.sum(grad_pre.astype(F32).reshape(TILE // 8, 8, TILE), axis=0)
    wl[0, :TILE] = self_local
    wl[1, :TILE] = neighbour_local
    wl[0, TILE:] = bias_local
    wl[1, TILE:] = bias_local
    w_core = send(wl.at[1 - k], wc, sibling)
    act_o[...] = (preact * sigma).astype(BF16)
    own_term = lax.dot_general(grad_pre, ws[...], LANES, preferred_element_type=F32)

    arrive([w_core])
    both = wl[k] + wc[...]
    for j in range(n_y):
        w1[j] = jnp.concatenate([both[j * wrows : (j + 1) * wrows], both[TILE:]], axis=0)
    wy_copies = [send(w1.at[lax.rem(y + d, n_y)], wy.at[d], at_y(d)) for d in y_far]

    arrive(a_copies)
    group_a = ga.at[pl.ds(y * n_z, n_z)]
    a_copies = [send(group_a, group_a, at_y(d)) for d in y_far]
    arrive(b_copies)
    group_b = gb.at[pl.ds(z * n_y, n_y)]
    b_copies = [send(group_b, group_b, at_z(d)) for d in z_far]

    arrive(wy_copies)
    summed = w1[y]
    for d in range(1, n_y):
        summed = summed + wy[d]
    w2[...] = summed
    wz_copies = [send(w2, wz.at[d], at_z(d)) for d in z_far]
    arrive(wz_copies)
    summed = w2[...]
    for d in range(1, n_z):
        summed = summed + wz[d]
    w3[...] = summed
    wx_copies = [send(w3, wx.at[d], at_q(d)) for d in q_far]

    arrive(a_copies)
    arrive(b_copies)

    def backward(g, acc):
        for u in range(STRETCH):
            s = g * STRETCH + u
            word = meta_s[2, s]
            slot, row = word & 127, (word >> 7) & 31
            target = jnp.concatenate([ga[row], gb[(row % n_z) * n_y + row // n_z]], axis=0)
            product = jnp.dot(bwd_adj[slot], target, preferred_element_type=F32)
            acc = jnp.where(word >= 4096, acc, 0.0) + product
            runs[s] = acc.astype(BF16)
        return acc

    lax.fori_loop(0, slots // STRETCH, backward, jnp.zeros((TILE, TILE), F32))

    def place_cols(j, _):
        word = meta_s[3, j]
        run = runs[word & 127]
        run = jnp.where(word >= 256, run, jnp.zeros_like(run))
        bp[(j % CORES) * n_q + j // CORES] = run
        return 0

    lax.fori_loop(0, n_src, place_cols, 0)

    b_core = {}
    for d in q_far + [0]:
        i = q_to(d)
        b_core[d] = send(bp.at[(1 - k) * n_q + i], br.at[i], sibling)
    back_copies = []
    for d in q_far:
        i = q_to(d)
        arrive([b_core[d]])
        bs[i] = (bp[k * n_q + i].astype(F32) + br[i].astype(F32)).astype(BF16)
        back_copies.append(send(bs.at[i], br2.at[d], at_q(d)))
    arrive([b_core[0]])
    feature_grad = own_term + (bp[k * n_q + q].astype(F32) + br[q].astype(F32))

    arrive(wx_copies)
    summed = w3[...]
    for d in range(1, n_q):
        summed = summed + wx[d]
    summed = summed * scaling
    wo[k * n_y + y] = summed[:wrows]
    own_w = wo.at[k * n_y + y]
    wo_copies = {d: send(own_w, own_w, at_y(d)) for d in y_far}
    wo_core = [send(own_w, own_w, sibling)]
    bg_o[...] = jnp.sum(summed[wrows:], axis=0, keepdims=True)

    for d in reversed(y_far):
        arrive([wo_copies[d]])
        block = wo.at[k * n_y + lax.rem(y + n_y - d, n_y)]
        wo_core.append(send(block, block, sibling))
    arrive(back_copies)
    for d in range(1, n_q):
        feature_grad = feature_grad + br2[d].astype(F32)
    fg_o[...] = feature_grad.astype(BF16)
    arrive(wo_core)
    sg_o[...] = wo[pl.ds(0, n_y)]
    ng_o[...] = wo[pl.ds(n_y, n_y)]
    for copy in started:
        copy.wait_send()


def hand_over(*refs):
    sources, results, sems = refs[:5], refs[5:10], refs[10]
    copies = [
        pltpu.make_async_copy(source, result, sems.at[i])
        for i, (source, result) in enumerate(zip(sources, results))
    ]
    for copy in copies:
        copy.start()
    for copy in copies:
        copy.wait()


def on_device(
    n_row,
    n_col,
    features,
    cotangent,
    self_weight,
    neighbour_weight,
    shift_bias,
    tile_rows,
    tile_cols,
    edge_targets,
    edge_sources,
):
    slots = edge_targets.shape[2]
    n_z = 4 if n_col >= 16 else 2
    n_y, n_q = n_col // n_z, n_row // CORES
    scaling = float((TILE * n_row * n_col) ** (-0.5))
    sizes = (n_q, n_y, n_z, slots, scaling)
    wrows = TILE // n_y
    n_dst, n_src = n_col, n_row
    copies = 7 * (n_y - 1) + 6 * (n_z - 1) + 3 * (n_q - 1) + 2 * n_q + n_y + 1
    scratch = [
        pltpu.VMEM((TILE, TILE), BF16),
        pltpu.VMEM((TILE, TILE), BF16),
        pltpu.VMEM((TILE, TILE), BF16),
        pltpu.VMEM((TILE, TILE), BF16),
        pltpu.VMEM((1, TILE), F32),
        pltpu.VMEM((1, slots), jnp.int32),
        pltpu.VMEM((1, slots), jnp.int32),
        pltpu.VMEM((slots, TILE), jnp.int32),
        pltpu.VMEM((slots, TILE), jnp.int32),
        pltpu.VMEM((slots, TILE, TILE), BF16),
        pltpu.VMEM((slots, TILE, TILE), BF16),
        pltpu.VMEM((slots, TILE, TILE), BF16),
        pltpu.VMEM((slots, TILE), F32),
        pltpu.VMEM((8, TILE), jnp.int32),
        pltpu.SMEM((8, TILE), jnp.int32),
        pltpu.VMEM((n_src, TILE, TILE), BF16),
        pltpu.VMEM((n_dst, HALF, TILE), BF16),
        pltpu.VMEM((n_dst, HALF, TILE), BF16),
        pltpu.VMEM((n_y, n_z, HALF, TILE), BF16),
        pltpu.VMEM((n_z, n_y, HALF, TILE), BF16),
        pltpu.VMEM((n_z, HALF, TILE), BF16),
        pltpu.VMEM((n_y, HALF, TILE), BF16),
        pltpu.VMEM((n_z, HALF, TILE), BF16),
        pltpu.VMEM((n_y, HALF, TILE), BF16),
        pltpu.VMEM((n_y, 8, TILE), F32),
        pltpu.VMEM((n_y, 8, TILE), F32),
        pltpu.VMEM((8, TILE), F32),
        pltpu.VMEM((n_z, 8, TILE), F32),
        pltpu.VMEM((n_dst, HALF, TILE), BF16),
        pltpu.VMEM((n_dst, HALF, TILE), BF16),
        pltpu.VMEM((n_src, TILE, TILE), BF16),
        pltpu.VMEM((n_q, TILE, TILE), BF16),
        pltpu.VMEM((n_q, TILE, TILE), BF16),
        pltpu.VMEM((n_q, TILE, TILE), BF16),
        pltpu.VMEM((CORES, TILE + 8, TILE), F32),
        pltpu.VMEM((TILE + 8, TILE), F32),
        pltpu.VMEM((n_y, wrows + 8, TILE), F32),
        pltpu.VMEM((n_q, wrows + 8, TILE), F32),
        pltpu.VMEM((wrows + 8, TILE), F32),
        pltpu.VMEM((n_y, wrows + 8, TILE), F32),
        pltpu.VMEM((wrows + 8, TILE), F32),
        pltpu.VMEM((n_z, wrows + 8, TILE), F32),
        pltpu.VMEM((CORES * n_y, wrows, TILE), F32),
        pltpu.SemaphoreType.DMA((copies,)),
        pltpu.SemaphoreType.DMA((copies,)),
        pltpu.SemaphoreType.DMA,
        pltpu.SemaphoreType.DMA((10,)),
    ]
    out_shape = (
        jax.ShapeDtypeStruct((TILE, TILE), BF16),
        jax.ShapeDtypeStruct((TILE, TILE), BF16),
        jax.ShapeDtypeStruct((n_y, wrows, TILE), F32),
        jax.ShapeDtypeStruct((n_y, wrows, TILE), F32),
        jax.ShapeDtypeStruct((1, TILE), F32),
    )
    operands = (
        features,
        cotangent,
        self_weight,
        neighbour_weight,
        shift_bias.reshape(1, TILE),
        tile_rows.reshape(1, slots),
        tile_cols.reshape(1, slots),
        edge_targets.reshape(slots, -1),
        edge_sources.reshape(slots, -1),
    )
    operands = [pltpu.with_memory_space_constraint(v, pltpu.HBM) for v in operands]
    results = pl.pallas_call(
        functools.partial(layer_kernel, sizes),
        out_shape=out_shape,
        in_specs=[pl.BlockSpec(memory_space=pltpu.HBM)] * 9,
        out_specs=(pl.BlockSpec(memory_space=pltpu.VMEM),) * 5,
        scratch_shapes=scratch,
        compiler_params=pltpu.CompilerParams(
            collective_id=0, has_side_effects=True, vmem_limit_bytes=44 * 2**20
        ),
        name="sage_layer",
    )(*operands)
    act, fg, sg, ng, bg = pl.pallas_call(
        hand_over,
        out_shape=out_shape,
        in_specs=[pl.BlockSpec(memory_space=pltpu.VMEM)] * 5,
        out_specs=(pl.BlockSpec(memory_space=pltpu.HBM),) * 5,
        scratch_shapes=[pltpu.SemaphoreType.DMA((5,))],
        compiler_params=pltpu.CompilerParams(vmem_limit_bytes=2 * 2**20),
        name="hand_over",
    )(*results)
    return act, fg, sg.reshape(TILE, TILE), ng.reshape(TILE, TILE), bg.reshape(TILE)


def solution(mesh):
    in_specs = (
        P(("row", "col"), None),
        P(("row", "col"), None),
        P(),
        P(),
        P(),
        P("row", "col", None),
        P("row", "col", None),
        P("row", "col", None, None),
        P("row", "col", None, None),
    )
    out_specs = (P(("row", "col"), None), P(("row", "col"), None), P(), P(), P())
    body = functools.partial(on_device, mesh.shape["row"], mesh.shape["col"])
    return jax.shard_map(
        body, mesh=mesh, in_specs=in_specs, out_specs=out_specs, check_vma=False
    )
```

```python
import functools

import jax
import jax.numpy as jnp
from jax import lax
from jax.experimental import pallas as pl
from jax.experimental.pallas import tpu as pltpu
from jax.sharding import PartitionSpec as P

TILE = 128
HALF = TILE // 2
CORES = 2
UNROLL = 16
STRETCH = 32
MESH = pl.DeviceIdType.MESH
F32 = jnp.float32
BF16 = jnp.bfloat16
LANES = (((1,), (1,)), ((), ()))
ROWS = (((0,), (0,)), ((), ()))


def far_first(n):
    return sorted(range(1, n), key=lambda d: -min(d, n - d))


def layer_kernel(
    sizes,
    feat_h,
    cot_h,
    ws_h,
    wn_h,
    bias_h,
    trow_h,
    tcol_h,
    et_h,
    es_h,
    act_o,
    fg_o,
    sg_o,
    ng_o,
    bg_o,
    feat,
    cot,
    ws,
    wn,
    bias,
    trow,
    tcol,
    et,
    es,
    fwd_adj,
    bwd_adj,
    runs,
    slot_counts,
    meta_v,
    meta_s,
    xb,
    pa,
    pb,
    ra,
    rb,
    sa,
    sb,
    ra2,
    rb2,
    deg,
    deg_r,
    deg2,
    deg2_r,
    ga,
    gb,
    bp,
    br,
    bs,
    br2,
    b0,
    b1,
    by,
    b2,
    bc,
    wl,
    wc,
    w0,
    w1,
    wx,
    w2,
    wy,
    w3,
    wz,
    w4,
    wh,
    wo,
    send_sems,
    recv_sems,
    meta_sem,
    in_sems,
):
    n_q, n_y, n_z, slots, scaling = sizes
    r = lax.axis_index("row")
    c = lax.axis_index("col")
    q, k = r // CORES, r % CORES
    y, z = c // n_z, c % n_z
    n_src = n_q * CORES
    n_dst = n_y * n_z
    wrows = TILE // n_y

    def at_y(d):
        return (r, lax.rem(y + d, n_y) * n_z + z)

    def at_z(d):
        return (r, y * n_z + lax.rem(z + d, n_z))

    n_x = n_q // 2
    x, h = q // 2, q % 2
    q_steps = [(dx, dh) for dx in range(n_x) for dh in range(2)]

    def q_to(d):
        return lax.rem(x + q_steps[d][0], n_x) * 2 + lax.rem(h + q_steps[d][1], 2)

    def q_from(d):
        return lax.rem(x + n_x - q_steps[d][0], n_x) * 2 + lax.rem(h + q_steps[d][1], 2)

    def at_q(d):
        return (q_to(d) * CORES + k, c)

    sibling = (q * CORES + 1 - k, c)

    used = [0]
    started = []

    def send(src, dst, device):
        i = used[0]
        used[0] += 1
        copy = pltpu.make_async_remote_copy(
            src_ref=src,
            dst_ref=dst,
            send_sem=send_sems.at[i],
            recv_sem=recv_sems.at[i],
            device_id=device,
            device_id_type=MESH,
        )
        copy.start()
        started.append(copy)
        return copy

    def arrive(copies):
        for copy in copies:
            copy.wait_recv()

    y_far, z_far = far_first(n_y), far_first(n_z)
    q_far = sorted(
        range(1, n_q),
        key=lambda d: -min(q_steps[d][0], n_x - q_steps[d][0]) - 4 * q_steps[d][1],
    )

    barrier = pltpu.get_barrier_semaphore()
    partners = [at_q(d) for d in q_far] + [at_y(d) for d in y_far]
    partners += [at_z(d) for d in z_far] + [sibling]
    for partner in partners:
        pl.semaphore_signal(barrier, inc=1, device_id=partner, device_id_type=MESH)

    local_in = []
    for i, (far, near) in enumerate(
        zip(
            (feat_h, trow_h, tcol_h, et_h, es_h, feat_h, ws_h, wn_h, bias_h, cot_h),
            (xb.at[k * n_q + q], trow, tcol, et, es, feat, ws, wn, bias, cot),
        )
    ):
        local_in.append(pltpu.make_async_copy(far, near, in_sems.at[i]))
        local_in[-1].start()

    pl.semaphore_wait(barrier, len(partners))

    mine = xb.at[k * n_q + q]
    x_copies = {d: send(feat_h, mine, at_q(d)) for d in q_far}
    x_core = [send(feat_h, mine, sibling)]
    for copy in local_in:
        copy.wait()

    sub = lax.broadcasted_iota(jnp.int32, (TILE, TILE), 0)
    lane = lax.broadcasted_iota(jnp.int32, (TILE, TILE), 1)
    rows_l = jnp.broadcast_to(trow[...], (TILE, TILE))
    cols_l = jnp.broadcast_to(tcol[...], (TILE, TILE))
    rows_s, cols_s = rows_l.T, cols_l.T

    def order(ids_l, ids_s, other_s):
        before = (ids_l < ids_s) | ((ids_l == ids_s) & (lane < sub))
        rank = jnp.sum(before.astype(jnp.int32), axis=1, keepdims=True)
        same = jnp.sum(((ids_l == ids_s) & (lane < sub)).astype(jnp.int32), axis=1, keepdims=True)
        packed = sub + other_s * 128 + jnp.minimum(same, 1) * 4096
        ordered = jnp.sum(jnp.where(rank == lane, packed, 0), axis=0, keepdims=True)
        upto = jnp.sum((ids_s <= lane).astype(jnp.int32), axis=0, keepdims=True)
        below = jnp.sum((ids_s < lane).astype(jnp.int32), axis=0, keepdims=True)
        ends = jnp.maximum(upto - 1, 0) + jnp.where(upto > below, 256, 0)
        return ordered, ends

    by_row, row_ends = order(rows_l, rows_s, cols_s)
    by_col, col_ends = order(cols_l, cols_s, rows_s)
    zero_row = jnp.zeros_like(by_row)
    meta_v[...] = jnp.concatenate([by_row, row_ends, by_col, col_ends] + [zero_row] * 4, axis=0)
    meta_copy = pltpu.make_async_copy(meta_v, meta_s, meta_sem)
    meta_copy.start()


    def build(g, _):
        base = pl.multiple_of(g * UNROLL, UNROLL)
        targets = et[pl.ds(base, UNROLL), :]
        sources = es[pl.ds(base, UNROLL), :]
        counts = []
        for u in range(UNROLL):
            hot_t = jnp.where(sub == targets[u : u + 1, :], 1.0, 0.0).astype(BF16)
            hot_s = jnp.where(sub == sources[u : u + 1, :], 1.0, 0.0).astype(BF16)
            fwd = lax.dot_general(hot_t, hot_s, LANES, preferred_element_type=F32)
            bwd = lax.dot_general(hot_s, hot_t, LANES, preferred_element_type=F32)
            fwd_adj[base + u] = fwd.astype(BF16)
            bwd_adj[base + u] = bwd.astype(BF16)
            counts.append(jnp.sum(bwd, axis=0, keepdims=True))
        slot_counts[pl.ds(base, UNROLL), :] = jnp.concatenate(counts, axis=0)
        return 0

    lax.fori_loop(0, slots // UNROLL, build, 0)

    for d in reversed(q_far):
        arrive([x_copies[d]])
        block = xb.at[k * n_q + q_from(d)]
        x_core.append(send(block, block, sibling))

    tile_sub = lax.broadcasted_iota(jnp.int32, (n_y * 8, TILE), 0)
    wanted = (tile_sub // 8) * n_z + tile_sub % 8
    hits = (jnp.broadcast_to(trow[...], (n_y * 8, TILE)) == wanted) & (tile_sub % 8 < n_z)
    partial = jnp.dot(
        jnp.where(hits, 1.0, 0.0).astype(BF16),
        slot_counts[...].astype(BF16),
        preferred_element_type=F32,
    )
    deg[...] = partial.reshape(n_y, 8, TILE)
    deg_copies = [send(deg.at[lax.rem(y + d, n_y)], deg_r.at[d], at_y(d)) for d in y_far]
    self_term = jnp.dot(feat[...], ws[...], preferred_element_type=F32)

    meta_copy.wait()
    arrive(x_core)

    def forward(g, acc):
        for u in range(STRETCH):
            s = g * STRETCH + u
            word = meta_s[0, s]
            slot, col = word & 127, (word >> 7) & 31
            source = xb[(col & 1) * n_q + (col >> 1)]
            product = jnp.dot(fwd_adj[slot], source, preferred_element_type=F32)
            acc = jnp.where(word >= 4096, acc, 0.0) + product
            runs[s] = acc.astype(BF16)
        return acc

    lax.fori_loop(0, slots // STRETCH, forward, jnp.zeros((TILE, TILE), F32))

    def place_rows(yy, _):
        for zz in range(n_z):
            word = meta_s[1, yy * n_z + zz]
            run = runs[word & 127]
            run = jnp.where(word >= 256, run, jnp.zeros_like(run))
            pa[yy * n_z + zz] = run[:HALF]
            pb[zz * n_y + yy] = run[HALF:]
        return 0

    lax.fori_loop(0, n_y, place_rows, 0)

    a_copies = [
        send(pa.at[pl.ds(lax.rem(y + d, n_y) * n_z, n_z)], ra.at[d], at_y(d)) for d in y_far
    ]
    b_copies = [
        send(pb.at[pl.ds(lax.rem(z + d, n_z) * n_y, n_y)], rb.at[d], at_z(d)) for d in z_far
    ]

    arrive(deg_copies)
    summed = deg[y]
    for d in range(1, n_y):
        summed = summed + deg_r[d]
    deg2[...] = summed
    deg2_copies = [send(deg2, deg2_r.at[d], at_z(d)) for d in z_far]

    total = pb[pl.ds(z * n_y, n_y)].astype(F32)
    for d, copy in zip(z_far, b_copies):
        arrive([copy])
        total = total + rb[d].astype(F32)
    sb[...] = total.astype(BF16)
    b2_copies = [send(sb.at[lax.rem(y + d, n_y)], rb2.at[d], at_y(d)) for d in y_far]
    total = pa[pl.ds(y * n_z, n_z)].astype(F32)
    for d, copy in zip(y_far, a_copies):
        arrive([copy])
        total = total + ra[d].astype(F32)
    sa[...] = total.astype(BF16)
    a2_copies = [send(sa.at[lax.rem(z + d, n_z)], ra2.at[d], at_z(d)) for d in z_far]

    arrive(deg2_copies)
    degree = deg2[...]
    for d in range(1, n_z):
        degree = degree + deg2_r[d]
    sub8 = lax.broadcasted_iota(jnp.int32, (8, TILE), 0)
    degree = jnp.sum(jnp.where(sub8 == z, degree, 0.0), axis=0, keepdims=True)
    inverse = 1.0 / (jnp.broadcast_to(degree, (TILE, TILE)).T + 1.0)

    arrive(a2_copies)
    upper = sa[z].astype(F32)
    for d in range(1, n_z):
        upper = upper + ra2[d].astype(F32)
    arrive(b2_copies)
    lower = sb[y].astype(F32)
    for d in range(1, n_y):
        lower = lower + rb2[d].astype(F32)
    neighbour_sum = jnp.concatenate([upper, lower], axis=0)

    aggregate = (neighbour_sum * inverse).astype(BF16)
    preact = self_term + jnp.dot(aggregate, wn[...], preferred_element_type=F32) + bias[...]
    sigma = jax.nn.sigmoid(preact)
    grad_pre = (cot[...].astype(F32) * sigma * (1.0 + preact * (1.0 - sigma))).astype(BF16)
    scaled = lax.dot_general(grad_pre, wn[...], LANES, preferred_element_type=F32) * inverse
    scaled = scaled.astype(BF16)

    ga[y * n_z + z] = scaled[:HALF]
    gb[z * n_y + y] = scaled[HALF:]
    own_a, own_b = ga.at[y * n_z + z], gb.at[z * n_y + y]
    b_copies = [send(own_b, own_b, at_y(d)) for d in y_far]
    a_copies = [send(own_a, own_a, at_z(d)) for d in z_far]

    self_local = lax.dot_general(feat[...], grad_pre, ROWS, preferred_element_type=F32)
    neighbour_local = lax.dot_general(aggregate, grad_pre, ROWS, preferred_element_type=F32)
    bias_local = jnp.sum(grad_pre.astype(F32).reshape(TILE // 8, 8, TILE), axis=0)
    wl[0] = self_local
    wl[1] = neighbour_local
    w_core = send(wl.at[1 - k], wc, sibling)
    b0[...] = bias_local
    act_o[...] = (preact * sigma).astype(BF16)
    own_term = lax.dot_general(grad_pre, ws[...], LANES, preferred_element_type=F32)

    arrive([w_core])
    w0[...] = (wl[k] + wc[...]).reshape(n_y, wrows, TILE)
    w1[...] = w0[...].astype(BF16)
    wy_copies = [send(w1.at[lax.rem(y + d, n_y)], wy.at[d], at_y(d)) for d in y_far]

    arrive(a_copies)
    group_a = ga.at[pl.ds(y * n_z, n_z)]
    a_copies = [send(group_a, group_a, at_y(d)) for d in y_far]
    arrive(b_copies)
    group_b = gb.at[pl.ds(z * n_y, n_y)]
    b_copies = [send(group_b, group_b, at_z(d)) for d in z_far]

    arrive(wy_copies)
    summed = w0[y]
    for d in range(1, n_y):
        summed = summed + wy[d].astype(F32)
    w2[...] = jnp.concatenate([summed, b0[...]], axis=0)
    wx_copies = [send(w2, wx.at[d], at_q(2 * d)) for d in range(1, n_x)]
    arrive(wx_copies)
    summed = w2[...]
    for d in range(1, n_x):
        summed = summed + wx[d]
    w3[...] = summed
    wz_copies = [send(w3, wz.at[d], at_z(d)) for d in z_far]

    arrive(a_copies)
    arrive(b_copies)
    arrive(wz_copies)
    summed = w3[...]
    for d in range(1, n_z):
        summed = summed + wz[d]
    w4[...] = summed
    w_flip = send(w4, wh, at_q(1))

    def backward(g, acc):
        for u in range(STRETCH):
            s = g * STRETCH + u
            word = meta_s[2, s]
            slot, row = word & 127, (word >> 7) & 31
            target = jnp.concatenate([ga[row], gb[(row % n_z) * n_y + row // n_z]], axis=0)
            product = jnp.dot(bwd_adj[slot], target, preferred_element_type=F32)
            acc = jnp.where(word >= 4096, acc, 0.0) + product
            runs[s] = acc.astype(BF16)
        return acc

    lax.fori_loop(0, slots // STRETCH, backward, jnp.zeros((TILE, TILE), F32))

    def place_cols(g, _):
        for u in range(4):
            word = meta_s[3, g * 4 + u]
            run = runs[word & 127]
            run = jnp.where(word >= 256, run, jnp.zeros_like(run))
            bp[(u % CORES) * n_q + g * 2 + u // CORES] = run
        return 0

    lax.fori_loop(0, n_src // 4, place_cols, 0)

    b_core = {}
    for d in q_far + [0]:
        i = q_to(d)
        b_core[d] = send(bp.at[(1 - k) * n_q + i], br.at[i], sibling)
    back_copies = []
    for d in q_far:
        i = q_to(d)
        arrive([b_core[d]])
        bs[i] = (bp[k * n_q + i].astype(F32) + br[i].astype(F32)).astype(BF16)
        back_copies.append(send(bs.at[i], br2.at[d], at_q(d)))
    arrive([b_core[0]])
    feature_grad = own_term + (bp[k * n_q + q].astype(F32) + br[q].astype(F32))

    arrive([w_flip])
    summed = (w4[...] + wh[...]) * scaling
    wo[k * n_y + y] = summed[:wrows]
    own_w = wo.at[k * n_y + y]
    wo_copies = {d: send(own_w, own_w, at_y(d)) for d in y_far}
    wo_core = [send(own_w, own_w, sibling)]
    b1[...] = summed[wrows:]
    by_copies = [send(b1, by.at[d], at_y(d)) for d in y_far]

    for d in reversed(y_far):
        arrive([wo_copies[d]])
        block = wo.at[k * n_y + lax.rem(y + n_y - d, n_y)]
        wo_core.append(send(block, block, sibling))
    arrive(by_copies)
    bias_sum = b1[...]
    for d in range(1, n_y):
        bias_sum = bias_sum + by[d]
    b2[...] = bias_sum
    b_last = send(b2, bc, sibling)
    for d, copy in zip(q_far, back_copies):
        arrive([copy])
        feature_grad = feature_grad + br2[d].astype(F32)
    fg_o[...] = feature_grad.astype(BF16)
    arrive([b_last])
    bg_o[...] = jnp.sum(b2[...] + bc[...], axis=0, keepdims=True)
    arrive(wo_core)
    sg_o[...] = wo[pl.ds(0, n_y)]
    ng_o[...] = wo[pl.ds(n_y, n_y)]
    for copy in started:
        copy.wait_send()
    assert used[0] == send_sems.shape[0]


def hand_over(*refs):
    sources, results, sems = refs[:5], refs[5:10], refs[10]
    copies = [
        pltpu.make_async_copy(source, result, sems.at[i])
        for i, (source, result) in enumerate(zip(sources, results))
    ]
    for copy in copies:
        copy.start()
    for copy in copies:
        copy.wait()


def on_device(
    n_row,
    n_col,
    features,
    cotangent,
    self_weight,
    neighbour_weight,
    shift_bias,
    tile_rows,
    tile_cols,
    edge_targets,
    edge_sources,
):
    slots = edge_targets.shape[2]
    n_z = 4 if n_col >= 16 else 2
    n_y, n_q = n_col // n_z, n_row // CORES
    scaling = float((TILE * n_row * n_col) ** (-0.5))
    sizes = (n_q, n_y, n_z, slots, scaling)
    wrows = TILE // n_y
    n_dst, n_src = n_col, n_row
    copies = 8 * (n_y - 1) + 6 * (n_z - 1) + 2 * (n_q - 1) + n_q // 2 + 2 * n_q + n_y + 2
    scratch = [
        pltpu.VMEM((TILE, TILE), BF16),
        pltpu.VMEM((TILE, TILE), BF16),
        pltpu.VMEM((TILE, TILE), BF16),
        pltpu.VMEM((TILE, TILE), BF16),
        pltpu.VMEM((1, TILE), F32),
        pltpu.VMEM((1, slots), jnp.int32),
        pltpu.VMEM((1, slots), jnp.int32),
        pltpu.VMEM((slots, TILE), jnp.int32),
        pltpu.VMEM((slots, TILE), jnp.int32),
        pltpu.VMEM((slots, TILE, TILE), BF16),
        pltpu.VMEM((slots, TILE, TILE), BF16),
        pltpu.VMEM((slots, TILE, TILE), BF16),
        pltpu.VMEM((slots, TILE), F32),
        pltpu.VMEM((8, TILE), jnp.int32),
        pltpu.SMEM((8, TILE), jnp.int32),
        pltpu.VMEM((n_src, TILE, TILE), BF16),
        pltpu.VMEM((n_dst, HALF, TILE), BF16),
        pltpu.VMEM((n_dst, HALF, TILE), BF16),
        pltpu.VMEM((n_y, n_z, HALF, TILE), BF16),
        pltpu.VMEM((n_z, n_y, HALF, TILE), BF16),
        pltpu.VMEM((n_z, HALF, TILE), BF16),
        pltpu.VMEM((n_y, HALF, TILE), BF16),
        pltpu.VMEM((n_z, HALF, TILE), BF16),
        pltpu.VMEM((n_y, HALF, TILE), BF16),
        pltpu.VMEM((n_y, 8, TILE), F32),
        pltpu.VMEM((n_y, 8, TILE), F32),
        pltpu.VMEM((8, TILE), F32),
        pltpu.VMEM((n_z, 8, TILE), F32),
        pltpu.VMEM((n_dst, HALF, TILE), BF16),
        pltpu.VMEM((n_dst, HALF, TILE), BF16),
        pltpu.VMEM((n_src, TILE, TILE), BF16),
        pltpu.VMEM((n_q, TILE, TILE), BF16),
        pltpu.VMEM((n_q, TILE, TILE), BF16),
        pltpu.VMEM((n_q, TILE, TILE), BF16),
        pltpu.VMEM((8, TILE), F32),
        pltpu.VMEM((8, TILE), F32),
        pltpu.VMEM((n_y, 8, TILE), F32),
        pltpu.VMEM((8, TILE), F32),
        pltpu.VMEM((8, TILE), F32),
        pltpu.VMEM((CORES, TILE, TILE), F32),
        pltpu.VMEM((TILE, TILE), F32),
        pltpu.VMEM((n_y, wrows, TILE), F32),
        pltpu.VMEM((n_y, wrows, TILE), BF16),
        pltpu.VMEM((n_q // 2, wrows + 8, TILE), F32),
        pltpu.VMEM((wrows + 8, TILE), F32),
        pltpu.VMEM((n_y, wrows, TILE), BF16),
        pltpu.VMEM((wrows + 8, TILE), F32),
        pltpu.VMEM((n_z, wrows + 8, TILE), F32),
        pltpu.VMEM((wrows + 8, TILE), F32),
        pltpu.VMEM((wrows + 8, TILE), F32),
        pltpu.VMEM((CORES * n_y, wrows, TILE), F32),
        pltpu.SemaphoreType.DMA((copies,)),
        pltpu.SemaphoreType.DMA((copies,)),
        pltpu.SemaphoreType.DMA,
        pltpu.SemaphoreType.DMA((10,)),
    ]
    out_shape = (
        jax.ShapeDtypeStruct((TILE, TILE), BF16),
        jax.ShapeDtypeStruct((TILE, TILE), BF16),
        jax.ShapeDtypeStruct((n_y, wrows, TILE), F32),
        jax.ShapeDtypeStruct((n_y, wrows, TILE), F32),
        jax.ShapeDtypeStruct((1, TILE), F32),
    )
    operands = (
        features,
        cotangent,
        self_weight,
        neighbour_weight,
        shift_bias.reshape(1, TILE),
        tile_rows.reshape(1, slots),
        tile_cols.reshape(1, slots),
        edge_targets.reshape(slots, -1),
        edge_sources.reshape(slots, -1),
    )
    operands = [pltpu.with_memory_space_constraint(v, pltpu.HBM) for v in operands]
    results = pl.pallas_call(
        functools.partial(layer_kernel, sizes),
        out_shape=out_shape,
        in_specs=[pl.BlockSpec(memory_space=pltpu.HBM)] * 9,
        out_specs=(pl.BlockSpec(memory_space=pltpu.VMEM),) * 5,
        scratch_shapes=scratch,
        compiler_params=pltpu.CompilerParams(
            collective_id=0, has_side_effects=True, vmem_limit_bytes=44 * 2**20
        ),
        name="sage_layer",
    )(*operands)
    act, fg, sg, ng, bg = pl.pallas_call(
        hand_over,
        out_shape=out_shape,
        in_specs=[pl.BlockSpec(memory_space=pltpu.VMEM)] * 5,
        out_specs=(pl.BlockSpec(memory_space=pltpu.HBM),) * 5,
        scratch_shapes=[pltpu.SemaphoreType.DMA((5,))],
        compiler_params=pltpu.CompilerParams(vmem_limit_bytes=2 * 2**20),
        name="hand_over",
    )(*results)
    return act, fg, sg.reshape(TILE, TILE), ng.reshape(TILE, TILE), bg.reshape(TILE)


def solution(mesh):
    in_specs = (
        P(("row", "col"), None),
        P(("row", "col"), None),
        P(),
        P(),
        P(),
        P("row", "col", None),
        P("row", "col", None),
        P("row", "col", None, None),
        P("row", "col", None, None),
    )
    out_specs = (P(("row", "col"), None), P(("row", "col"), None), P(), P(), P())
    body = functools.partial(on_device, mesh.shape["row"], mesh.shape["col"])
    return jax.shard_map(
        body, mesh=mesh, in_specs=in_specs, out_specs=out_specs, check_vma=False
    )
```

```python
import functools

import jax
import jax.numpy as jnp
from jax import lax
from jax.experimental import pallas as pl
from jax.experimental.pallas import tpu as pltpu
from jax.sharding import PartitionSpec as P

TILE = 128
HALF = TILE // 2
CORES = 2
UNROLL = 16
STRETCH = 32
MESH = pl.DeviceIdType.MESH
F32 = jnp.float32
BF16 = jnp.bfloat16
LANES = (((1,), (1,)), ((), ()))
ROWS = (((0,), (0,)), ((), ()))


def far_first(n):
    return sorted(range(1, n), key=lambda d: -min(d, n - d))


def layer_kernel(
    sizes,
    feat_h,
    cot_h,
    ws_h,
    wn_h,
    bias_h,
    trow_h,
    tcol_h,
    et_h,
    es_h,
    act_o,
    fg_o,
    sg_o,
    ng_o,
    bg_o,
    feat,
    cot,
    ws,
    wn,
    bias,
    trow,
    tcol,
    et,
    es,
    fwd_adj,
    bwd_adj,
    runs,
    slot_counts,
    meta_v,
    meta_s,
    xb,
    pa,
    pb,
    ra,
    rb,
    sa,
    sb,
    ra2,
    rb2,
    deg,
    deg_r,
    deg2,
    deg2_r,
    ga,
    gb,
    bp,
    br,
    bs,
    br2,
    b0,
    b1,
    by,
    b2,
    bc,
    wl,
    wc,
    w0,
    w1,
    wx,
    w2,
    wy,
    w3,
    wz,
    w4,
    wh,
    wo,
    send_sems,
    recv_sems,
    meta_sem,
    in_sems,
):
    n_q, n_y, n_z, slots, scaling = sizes
    r = lax.axis_index("row")
    c = lax.axis_index("col")
    q, k = r // CORES, r % CORES
    y, z = c // n_z, c % n_z
    n_src = n_q * CORES
    n_dst = n_y * n_z
    wrows = TILE // n_y

    def at_y(d):
        return (r, lax.rem(y + d, n_y) * n_z + z)

    def at_z(d):
        return (r, y * n_z + lax.rem(z + d, n_z))

    n_x = n_q // 2
    x, h = q // 2, q % 2
    q_steps = [(dx, dh) for dx in range(n_x) for dh in range(2)]

    def q_to(d):
        return lax.rem(x + q_steps[d][0], n_x) * 2 + lax.rem(h + q_steps[d][1], 2)

    def q_from(d):
        return lax.rem(x + n_x - q_steps[d][0], n_x) * 2 + lax.rem(h + q_steps[d][1], 2)

    def at_q(d):
        return (q_to(d) * CORES + k, c)

    sibling = (q * CORES + 1 - k, c)

    used = [0]
    started = []

    def send(src, dst, device):
        i = used[0]
        used[0] += 1
        copy = pltpu.make_async_remote_copy(
            src_ref=src,
            dst_ref=dst,
            send_sem=send_sems.at[i],
            recv_sem=recv_sems.at[i],
            device_id=device,
            device_id_type=MESH,
        )
        copy.start()
        started.append(copy)
        return copy

    def arrive(copies):
        for copy in copies:
            copy.wait_recv()

    y_far, z_far = far_first(n_y), far_first(n_z)
    q_far = sorted(
        range(1, n_q),
        key=lambda d: -min(q_steps[d][0], n_x - q_steps[d][0]) - 4 * q_steps[d][1],
    )

    barrier = pltpu.get_barrier_semaphore()
    partners = [at_q(d) for d in q_far] + [at_y(d) for d in y_far]
    partners += [at_z(d) for d in z_far] + [sibling]
    for partner in partners:
        pl.semaphore_signal(barrier, inc=1, device_id=partner, device_id_type=MESH)

    local_in = []
    for i, (far, near) in enumerate(
        zip(
            (feat_h, trow_h, tcol_h, et_h, es_h, feat_h, ws_h, wn_h, bias_h, cot_h),
            (xb.at[k * n_q + q], trow, tcol, et, es, feat, ws, wn, bias, cot),
        )
    ):
        local_in.append(pltpu.make_async_copy(far, near, in_sems.at[i]))
        local_in[-1].start()

    pl.semaphore_wait(barrier, len(partners))

    mine = xb.at[k * n_q + q]
    x_copies = {d: send(feat_h, mine, at_q(d)) for d in q_far}
    x_core = [send(feat_h, mine, sibling)]
    for copy in local_in:
        copy.wait()

    sub = lax.broadcasted_iota(jnp.int32, (TILE, TILE), 0)
    lane = lax.broadcasted_iota(jnp.int32, (TILE, TILE), 1)
    rows_l = jnp.broadcast_to(trow[...], (TILE, TILE))
    cols_l = jnp.broadcast_to(tcol[...], (TILE, TILE))
    rows_s, cols_s = rows_l.T, cols_l.T

    def order(ids_l, ids_s, other_s):
        before = (ids_l < ids_s) | ((ids_l == ids_s) & (lane < sub))
        rank = jnp.sum(before.astype(jnp.int32), axis=1, keepdims=True)
        same = jnp.sum(((ids_l == ids_s) & (lane < sub)).astype(jnp.int32), axis=1, keepdims=True)
        packed = sub + other_s * 128 + jnp.minimum(same, 1) * 4096
        ordered = jnp.sum(jnp.where(rank == lane, packed, 0), axis=0, keepdims=True)
        upto = jnp.sum((ids_s <= lane).astype(jnp.int32), axis=0, keepdims=True)
        below = jnp.sum((ids_s < lane).astype(jnp.int32), axis=0, keepdims=True)
        ends = jnp.maximum(upto - 1, 0) + jnp.where(upto > below, 256, 0)
        return ordered, ends

    by_row, row_ends = order(rows_l, rows_s, cols_s)
    by_col, col_ends = order(cols_l, cols_s, rows_s)
    zero_row = jnp.zeros_like(by_row)
    meta_v[...] = jnp.concatenate([by_row, row_ends, by_col, col_ends] + [zero_row] * 4, axis=0)
    meta_copy = pltpu.make_async_copy(meta_v, meta_s, meta_sem)
    meta_copy.start()


    def build(g, _):
        base = pl.multiple_of(g * UNROLL, UNROLL)
        targets = et[pl.ds(base, UNROLL), :]
        sources = es[pl.ds(base, UNROLL), :]
        counts = []
        for u in range(UNROLL):
            hot_t = jnp.where(sub == targets[u : u + 1, :], 1.0, 0.0).astype(BF16)
            hot_s = jnp.where(sub == sources[u : u + 1, :], 1.0, 0.0).astype(BF16)
            fwd = lax.dot_general(hot_t, hot_s, LANES, preferred_element_type=F32)
            bwd = lax.dot_general(hot_s, hot_t, LANES, preferred_element_type=F32)
            fwd_adj[base + u] = fwd.astype(BF16)
            bwd_adj[base + u] = bwd.astype(BF16)
            counts.append(jnp.sum(bwd, axis=0, keepdims=True))
        slot_counts[pl.ds(base, UNROLL), :] = jnp.concatenate(counts, axis=0)
        return 0

    lax.fori_loop(0, slots // UNROLL, build, 0)

    for d in reversed(q_far):
        arrive([x_copies[d]])
        block = xb.at[k * n_q + q_from(d)]
        x_core.append(send(block, block, sibling))

    tile_sub = lax.broadcasted_iota(jnp.int32, (n_y * 8, TILE), 0)
    wanted = (tile_sub // 8) * n_z + tile_sub % 8
    hits = (jnp.broadcast_to(trow[...], (n_y * 8, TILE)) == wanted) & (tile_sub % 8 < n_z)
    partial = jnp.dot(
        jnp.where(hits, 1.0, 0.0).astype(BF16),
        slot_counts[...].astype(BF16),
        preferred_element_type=F32,
    )
    deg[...] = partial.reshape(n_y, 8, TILE)
    deg_copies = [send(deg.at[lax.rem(y + d, n_y)], deg_r.at[d], at_y(d)) for d in y_far]
    self_term = jnp.dot(feat[...], ws[...], preferred_element_type=F32)

    meta_copy.wait()
    arrive(x_core)

    def forward(g, acc):
        for u in range(STRETCH):
            s = g * STRETCH + u
            word = meta_s[0, s]
            slot, col = word & 127, (word >> 7) & 31
            source = xb[(col & 1) * n_q + (col >> 1)]
            product = jnp.dot(fwd_adj[slot], source, preferred_element_type=F32)
            acc = jnp.where(word >= 4096, acc, 0.0) + product
            runs[s] = acc.astype(BF16)
        return acc

    lax.fori_loop(0, slots // STRETCH, forward, jnp.zeros((TILE, TILE), F32))

    def place_rows(yy, _):
        for zz in range(n_z):
            word = meta_s[1, yy * n_z + zz]
            run = runs[word & 127]
            run = jnp.where(word >= 256, run, jnp.zeros_like(run))
            pa[yy * n_z + zz] = run[:HALF]
            pb[zz * n_y + yy] = run[HALF:]
        return 0

    lax.fori_loop(0, n_y, place_rows, 0)

    a_copies = [
        send(pa.at[pl.ds(lax.rem(y + d, n_y) * n_z, n_z)], ra.at[d], at_y(d)) for d in y_far
    ]
    b_copies = [
        send(pb.at[pl.ds(lax.rem(z + d, n_z) * n_y, n_y)], rb.at[d], at_z(d)) for d in z_far
    ]

    arrive(deg_copies)
    summed = deg[y]
    for d in range(1, n_y):
        summed = summed + deg_r[d]
    deg2[...] = summed
    deg2_copies = [send(deg2, deg2_r.at[d], at_z(d)) for d in z_far]

    total = pb[pl.ds(z * n_y, n_y)].astype(F32)
    for d, copy in zip(z_far, b_copies):
        arrive([copy])
        total = total + rb[d].astype(F32)
    sb[...] = total.astype(BF16)
    b2_copies = [send(sb.at[lax.rem(y + d, n_y)], rb2.at[d], at_y(d)) for d in y_far]
    total = pa[pl.ds(y * n_z, n_z)].astype(F32)
    for d, copy in zip(y_far, a_copies):
        arrive([copy])
        total = total + ra[d].astype(F32)
    sa[...] = total.astype(BF16)
    a2_copies = [send(sa.at[lax.rem(z + d, n_z)], ra2.at[d], at_z(d)) for d in z_far]

    arrive(deg2_copies)
    degree = deg2[...]
    for d in range(1, n_z):
        degree = degree + deg2_r[d]
    sub8 = lax.broadcasted_iota(jnp.int32, (8, TILE), 0)
    degree = jnp.sum(jnp.where(sub8 == z, degree, 0.0), axis=0, keepdims=True)
    inverse = 1.0 / (jnp.broadcast_to(degree, (TILE, TILE)).T + 1.0)

    arrive(a2_copies)
    upper = sa[z].astype(F32)
    for d in range(1, n_z):
        upper = upper + ra2[d].astype(F32)
    arrive(b2_copies)
    lower = sb[y].astype(F32)
    for d in range(1, n_y):
        lower = lower + rb2[d].astype(F32)
    neighbour_sum = jnp.concatenate([upper, lower], axis=0)

    aggregate = (neighbour_sum * inverse).astype(BF16)
    preact = self_term + jnp.dot(aggregate, wn[...], preferred_element_type=F32) + bias[...]
    sigma = jax.nn.sigmoid(preact)
    grad_pre = (cot[...].astype(F32) * sigma * (1.0 + preact * (1.0 - sigma))).astype(BF16)
    scaled = lax.dot_general(grad_pre, wn[...], LANES, preferred_element_type=F32) * inverse
    scaled = scaled.astype(BF16)

    ga[y * n_z + z] = scaled[:HALF]
    gb[z * n_y + y] = scaled[HALF:]
    own_a, own_b = ga.at[y * n_z + z], gb.at[z * n_y + y]
    b_copies = [send(own_b, own_b, at_y(d)) for d in y_far]
    a_copies = [send(own_a, own_a, at_z(d)) for d in z_far]

    self_local = lax.dot_general(feat[...], grad_pre, ROWS, preferred_element_type=F32)
    neighbour_local = lax.dot_general(aggregate, grad_pre, ROWS, preferred_element_type=F32)
    bias_local = jnp.sum(grad_pre.astype(F32).reshape(TILE // 8, 8, TILE), axis=0)
    wl[0] = self_local
    wl[1] = neighbour_local
    w_core = send(wl.at[1 - k], wc, sibling)
    b0[...] = bias_local

    arrive([w_core])
    w0[...] = (wl[k] + wc[...]).reshape(n_y, wrows, TILE)
    w1[...] = w0[...].astype(BF16)
    wy_copies = [send(w1.at[lax.rem(y + d, n_y)], wy.at[d], at_y(d)) for d in y_far]

    arrive(a_copies)
    group_a = ga.at[pl.ds(y * n_z, n_z)]
    a_copies = [send(group_a, group_a, at_y(d)) for d in y_far]
    arrive(b_copies)
    group_b = gb.at[pl.ds(z * n_y, n_y)]
    b_copies = [send(group_b, group_b, at_z(d)) for d in z_far]
    act_o[...] = (preact * sigma).astype(BF16)
    own_term = lax.dot_general(grad_pre, ws[...], LANES, preferred_element_type=F32)

    arrive(wy_copies)
    summed = w0[y]
    for d in range(1, n_y):
        summed = summed + wy[d].astype(F32)
    w2[...] = jnp.concatenate([summed, b0[...]], axis=0)
    wx_copies = [send(w2, wx.at[d], at_q(2 * d)) for d in range(1, n_x)]
    arrive(wx_copies)
    summed = w2[...]
    for d in range(1, n_x):
        summed = summed + wx[d]
    w3[...] = summed
    wz_copies = [send(w3, wz.at[d], at_z(d)) for d in z_far]

    arrive(a_copies)
    arrive(b_copies)
    arrive(wz_copies)
    summed = w3[...]
    for d in range(1, n_z):
        summed = summed + wz[d]
    w4[...] = summed
    w_flip = send(w4, wh, at_q(1))

    def backward(g, acc):
        for u in range(STRETCH):
            s = g * STRETCH + u
            word = meta_s[2, s]
            slot, row = word & 127, (word >> 7) & 31
            target = jnp.concatenate([ga[row], gb[(row % n_z) * n_y + row // n_z]], axis=0)
            product = jnp.dot(bwd_adj[slot], target, preferred_element_type=F32)
            acc = jnp.where(word >= 4096, acc, 0.0) + product
            runs[s] = acc.astype(BF16)
        return acc

    lax.fori_loop(0, slots // STRETCH, backward, jnp.zeros((TILE, TILE), F32))

    def place_cols(g, _):
        for u in range(4):
            word = meta_s[3, g * 4 + u]
            run = runs[word & 127]
            run = jnp.where(word >= 256, run, jnp.zeros_like(run))
            bp[(u % CORES) * n_q + g * 2 + u // CORES] = run
        return 0

    lax.fori_loop(0, n_src // 4, place_cols, 0)

    b_core = {}
    for d in q_far + [0]:
        i = q_to(d)
        b_core[d] = send(bp.at[(1 - k) * n_q + i], br.at[i], sibling)
    back_copies = []
    for d in q_far:
        i = q_to(d)
        arrive([b_core[d]])
        bs[i] = (bp[k * n_q + i].astype(F32) + br[i].astype(F32)).astype(BF16)
        back_copies.append(send(bs.at[i], br2.at[d], at_q(d)))
    arrive([b_core[0]])
    feature_grad = own_term + (bp[k * n_q + q].astype(F32) + br[q].astype(F32))

    arrive([w_flip])
    summed = (w4[...] + wh[...]) * scaling
    wo[k * n_y + y] = summed[:wrows]
    own_w = wo.at[k * n_y + y]
    wo_copies = {d: send(own_w, own_w, at_y(d)) for d in y_far}
    wo_core = [send(own_w, own_w, sibling)]
    b1[...] = summed[wrows:]
    by_copies = [send(b1, by.at[d], at_y(d)) for d in y_far]

    for d in reversed(y_far):
        arrive([wo_copies[d]])
        block = wo.at[k * n_y + lax.rem(y + n_y - d, n_y)]
        wo_core.append(send(block, block, sibling))
    arrive(by_copies)
    bias_sum = b1[...]
    for d in range(1, n_y):
        bias_sum = bias_sum + by[d]
    b2[...] = bias_sum
    b_last = send(b2, bc, sibling)
    for d, copy in zip(q_far, back_copies):
        arrive([copy])
        feature_grad = feature_grad + br2[d].astype(F32)
    fg_o[...] = feature_grad.astype(BF16)
    arrive([b_last])
    bg_o[...] = jnp.sum(b2[...] + bc[...], axis=0, keepdims=True)
    arrive(wo_core)
    sg_o[...] = wo[pl.ds(0, n_y)]
    ng_o[...] = wo[pl.ds(n_y, n_y)]
    for copy in started:
        copy.wait_send()
    assert used[0] == send_sems.shape[0]


def hand_over(*refs):
    sources, results, sems = refs[:5], refs[5:10], refs[10]
    copies = [
        pltpu.make_async_copy(source, result, sems.at[i])
        for i, (source, result) in enumerate(zip(sources, results))
    ]
    for copy in copies:
        copy.start()
    for copy in copies:
        copy.wait()


def on_device(
    n_row,
    n_col,
    features,
    cotangent,
    self_weight,
    neighbour_weight,
    shift_bias,
    tile_rows,
    tile_cols,
    edge_targets,
    edge_sources,
):
    slots = edge_targets.shape[2]
    n_z = 4 if n_col >= 16 else 2
    n_y, n_q = n_col // n_z, n_row // CORES
    scaling = float((TILE * n_row * n_col) ** (-0.5))
    sizes = (n_q, n_y, n_z, slots, scaling)
    wrows = TILE // n_y
    n_dst, n_src = n_col, n_row
    copies = 8 * (n_y - 1) + 6 * (n_z - 1) + 2 * (n_q - 1) + n_q // 2 + 2 * n_q + n_y + 2
    scratch = [
        pltpu.VMEM((TILE, TILE), BF16),
        pltpu.VMEM((TILE, TILE), BF16),
        pltpu.VMEM((TILE, TILE), BF16),
        pltpu.VMEM((TILE, TILE), BF16),
        pltpu.VMEM((1, TILE), F32),
        pltpu.VMEM((1, slots), jnp.int32),
        pltpu.VMEM((1, slots), jnp.int32),
        pltpu.VMEM((slots, TILE), jnp.int32),
        pltpu.VMEM((slots, TILE), jnp.int32),
        pltpu.VMEM((slots, TILE, TILE), BF16),
        pltpu.VMEM((slots, TILE, TILE), BF16),
        pltpu.VMEM((slots, TILE, TILE), BF16),
        pltpu.VMEM((slots, TILE), F32),
        pltpu.VMEM((8, TILE), jnp.int32),
        pltpu.SMEM((8, TILE), jnp.int32),
        pltpu.VMEM((n_src, TILE, TILE), BF16),
        pltpu.VMEM((n_dst, HALF, TILE), BF16),
        pltpu.VMEM((n_dst, HALF, TILE), BF16),
        pltpu.VMEM((n_y, n_z, HALF, TILE), BF16),
        pltpu.VMEM((n_z, n_y, HALF, TILE), BF16),
        pltpu.VMEM((n_z, HALF, TILE), BF16),
        pltpu.VMEM((n_y, HALF, TILE), BF16),
        pltpu.VMEM((n_z, HALF, TILE), BF16),
        pltpu.VMEM((n_y, HALF, TILE), BF16),
        pltpu.VMEM((n_y, 8, TILE), F32),
        pltpu.VMEM((n_y, 8, TILE), F32),
        pltpu.VMEM((8, TILE), F32),
        pltpu.VMEM((n_z, 8, TILE), F32),
        pltpu.VMEM((n_dst, HALF, TILE), BF16),
        pltpu.VMEM((n_dst, HALF, TILE), BF16),
        pltpu.VMEM((n_src, TILE, TILE), BF16),
        pltpu.VMEM((n_q, TILE, TILE), BF16),
        pltpu.VMEM((n_q, TILE, TILE), BF16),
        pltpu.VMEM((n_q, TILE, TILE), BF16),
        pltpu.VMEM((8, TILE), F32),
        pltpu.VMEM((8, TILE), F32),
        pltpu.VMEM((n_y, 8, TILE), F32),
        pltpu.VMEM((8, TILE), F32),
        pltpu.VMEM((8, TILE), F32),
        pltpu.VMEM((CORES, TILE, TILE), F32),
        pltpu.VMEM((TILE, TILE), F32),
        pltpu.VMEM((n_y, wrows, TILE), F32),
        pltpu.VMEM((n_y, wrows, TILE), BF16),
        pltpu.VMEM((n_q // 2, wrows + 8, TILE), F32),
        pltpu.VMEM((wrows + 8, TILE), F32),
        pltpu.VMEM((n_y, wrows, TILE), BF16),
        pltpu.VMEM((wrows + 8, TILE), F32),
        pltpu.VMEM((n_z, wrows + 8, TILE), F32),
        pltpu.VMEM((wrows + 8, TILE), F32),
        pltpu.VMEM((wrows + 8, TILE), F32),
        pltpu.VMEM((CORES * n_y, wrows, TILE), F32),
        pltpu.SemaphoreType.DMA((copies,)),
        pltpu.SemaphoreType.DMA((copies,)),
        pltpu.SemaphoreType.DMA,
        pltpu.SemaphoreType.DMA((10,)),
    ]
    out_shape = (
        jax.ShapeDtypeStruct((TILE, TILE), BF16),
        jax.ShapeDtypeStruct((TILE, TILE), BF16),
        jax.ShapeDtypeStruct((n_y, wrows, TILE), F32),
        jax.ShapeDtypeStruct((n_y, wrows, TILE), F32),
        jax.ShapeDtypeStruct((1, TILE), F32),
    )
    operands = (
        features,
        cotangent,
        self_weight,
        neighbour_weight,
        shift_bias.reshape(1, TILE),
        tile_rows.reshape(1, slots),
        tile_cols.reshape(1, slots),
        edge_targets.reshape(slots, -1),
        edge_sources.reshape(slots, -1),
    )
    operands = [pltpu.with_memory_space_constraint(v, pltpu.HBM) for v in operands]
    results = pl.pallas_call(
        functools.partial(layer_kernel, sizes),
        out_shape=out_shape,
        in_specs=[pl.BlockSpec(memory_space=pltpu.HBM)] * 9,
        out_specs=(pl.BlockSpec(memory_space=pltpu.VMEM),) * 5,
        scratch_shapes=scratch,
        compiler_params=pltpu.CompilerParams(
            collective_id=0, has_side_effects=True, vmem_limit_bytes=44 * 2**20
        ),
        name="sage_layer",
    )(*operands)
    act, fg, sg, ng, bg = pl.pallas_call(
        hand_over,
        out_shape=out_shape,
        in_specs=[pl.BlockSpec(memory_space=pltpu.VMEM)] * 5,
        out_specs=(pl.BlockSpec(memory_space=pltpu.HBM),) * 5,
        scratch_shapes=[pltpu.SemaphoreType.DMA((5,))],
        compiler_params=pltpu.CompilerParams(vmem_limit_bytes=2 * 2**20),
        name="hand_over",
    )(*results)
    return act, fg, sg.reshape(TILE, TILE), ng.reshape(TILE, TILE), bg.reshape(TILE)


def solution(mesh):
    in_specs = (
        P(("row", "col"), None),
        P(("row", "col"), None),
        P(),
        P(),
        P(),
        P("row", "col", None),
        P("row", "col", None),
        P("row", "col", None, None),
        P("row", "col", None, None),
    )
    out_specs = (P(("row", "col"), None), P(("row", "col"), None), P(), P(), P())
    body = functools.partial(on_device, mesh.shape["row"], mesh.shape["col"])
    return jax.shard_map(
        body, mesh=mesh, in_specs=in_specs, out_specs=out_specs, check_vma=False
    )
```
